128 devices in a mesh: dp: 8 (over x, core), mp: 16 (over z, y).
Axes of the slice: x: 4, y: 4, z: 4, core: 2. Of those that a mesh axis runs over, the one named last changes fastest.
Arguments:
- sensitivity: bfloat16 [8192, 32, 1024], P('dp', 'mp'), may hold values from -0.03125 to 0.03125
- observed: float32 [8192], P('dp'), may hold values from -6 to 6
- row_weight: float32 [8192], P('dp'), may hold values from 1 to 8
- model: float32 [2, 32, 1024], P(None, 'mp'), may hold values from -3 to 3
- smooth_weight: float32 [32, 1024], P('mp'), may hold values from 0.5 to 2
- active: int32 [2, 32, 1024], P(None, 'mp'), may hold values 0 or 1
Outputs:
- update: float32 [2, 32, 1024], P(None, 'mp')
- cg_residual: float32 [2, 32, 1024], P(None, 'mp')
The draws below stay inside these ranges and needn't reach their ends.
All inputs are finite; a program needn't handle non-finite values. No bound on the sum of `active` on one device may be relied on, other than what follows from the above.
Results may differ from the reference program's by a relative error of at most 0.018.
Values sent between devices are 32-bit elements; how exact they have to be, the bound alone decides.
A program may use at most 64 MiB of HBM per device.

```python
import math
import jax
import jax.numpy as jnp

GY = 64
GZ = 16
ITERS = 4
GX = 32
ROWS = 8192


def touch_ends(values, stream_key, low, top_value):
    longest = values.shape.index(max(values.shape))
    spots = []
    for shift in (0, 1):
        where = [jax.random.randint(jax.random.fold_in(stream_key, axis), (), 0, length) for axis, length in enumerate(values.shape)]
        where[longest] = (where[longest] + shift) % values.shape[longest]
        spots.append(tuple(where))
    return values.at[spots[0]].set(low).at[spots[1]].set(top_value)


def shard_levels(rng, dims, shards, low, high):
    def one(dim, blocks):
        draws = jax.random.uniform(jax.random.fold_in(jax.random.fold_in(rng, 6), dim), (blocks,), jnp.float32, low / len(shards), high / len(shards))
        return jnp.repeat(jnp.exp(draws), dims[dim] // blocks).reshape((-1,) + (1,) * (len(dims) - dim - 1))

    loudness = one(*shards[0])
    for cut in shards[1:]:
        loudness = loudness * one(*cut)
    return loudness


def noise(own_key, shape, spread, limit, cuts=(), held_as=jnp.bfloat16):
    values = spread * jax.random.normal(own_key, shape, jnp.float32)
    if cuts:
        values = values * shard_levels(own_key, shape, cuts, -0.22, 0.18)
    return jnp.clip(values, -limit, limit).astype(held_as)


def setup_inputs(seed: int = 0) -> dict:
    streams_of = jax.random.split(jax.random.key(seed), 7)
    return {
        "sensitivity": noise(streams_of[0], (ROWS, GX, GY * GZ), (GX * GY * GZ) ** -0.5, 0.03125, ((0, 8), (1, 16))),
        "observed": noise(streams_of[1], (ROWS,), 1.0, 6.0, ((0, 8),), jnp.float32),
        "row_weight": jnp.clip(jnp.exp(math.log(8.0) - 2.0794415 * jax.random.uniform(streams_of[2], (ROWS,), jnp.float32) ** shard_levels(streams_of[2], (ROWS,), ((0, 8),), -0.2, 0.2)), 1.0, 8.0),
        "model": noise(streams_of[3], (2, GX, GY * GZ), 0.5, 3.0, ((1, 16),), jnp.float32),
        "smooth_weight": jnp.clip(jnp.exp(math.log(2.0) - 1.3862944 * jax.random.uniform(streams_of[4], (GX, GY * GZ), jnp.float32) ** shard_levels(streams_of[4], (GX, GY * GZ), ((0, 16),), -0.2, 0.2)), 0.5, 2.0),
        "active": touch_ends((jax.random.randint(streams_of[5], (2, GX, GY * GZ), 0, 4) < 1).astype(jnp.int32), jax.random.fold_in(streams_of[5], 1), 0, 1),
    }


SMOOTHING = 0.25
COUPLING = 0.5


def inner_sum(field, column_len):
    width = field.shape[-1]
    position = jnp.arange(width) % column_len
    blank_one = jnp.zeros_like(field[..., :1])
    blank_col = jnp.zeros_like(field[..., :column_len])
    later = jnp.where(position != column_len - 1, jnp.concatenate([field[..., 1:], blank_one], -1), 0.0)
    earlier = jnp.where(position != 0, jnp.concatenate([blank_one, field[..., :-1]], -1), 0.0)
    ahead = jnp.concatenate([field[..., column_len:], blank_col], -1)
    behind = jnp.concatenate([blank_col, field[..., :-column_len]], -1)
    return later + earlier + ahead + behind


def operate(field, smooth_weight):
    padded = jnp.pad(field, ((0, 0), (1, 1), (0, 0)))
    beside = padded[:, 2:] + padded[:, :-2] + inner_sum(field, GZ)
    return smooth_weight * field + SMOOTHING * (6.0 * field - beside) + COUPLING * (field - field[::-1])


def reference(sensitivity, observed, row_weight, model, smooth_weight, active):
    rows = sensitivity.shape[0]
    split = rows * 3 // 4
    matrix = sensitivity.reshape(rows, -1)
    upper = matrix[:split]
    lower = matrix[split:]
    free_mask = 1.0 - active.astype(jnp.float32)
    cell_shape = model.shape

    def forward(field):
        flattened = field.reshape(2, -1).astype(jnp.bfloat16)
        return jnp.concatenate([jnp.dot(upper, flattened[0], preferred_element_type=jnp.float32),
                                jnp.dot(lower, flattened[1], preferred_element_type=jnp.float32)])

    def adjoint(values, regular):
        scaled = (row_weight * values).astype(jnp.bfloat16)
        summed = jnp.stack([jnp.dot(scaled[:split], upper, preferred_element_type=jnp.float32),
                            jnp.dot(scaled[split:], lower, preferred_element_type=jnp.float32)])
        return free_mask * (summed.reshape(cell_shape) + regular)

    residual = -adjoint(forward(model) - observed, operate(model, smooth_weight))
    direction = residual
    solution = jnp.zeros_like(model)
    norm_now = jnp.sum(residual * residual)
    for step in range(ITERS):
        image = adjoint(forward(direction), operate(direction, smooth_weight))
        step_len = norm_now / jnp.sum(direction * image)
        solution = solution + step_len * direction
        residual = residual - step_len * image
        norm_next = jnp.sum(residual * residual)
        direction = residual + (norm_next / norm_now) * direction
        norm_now = norm_next
    return solution, residual
```

```python
import functools

import jax
import jax.numpy as jnp
from jax import lax
from jax.experimental import pallas as pl
from jax.experimental.pallas import tpu as pltpu
from jax.sharding import PartitionSpec as P

MESH = pl.DeviceIdType.MESH
F32 = jnp.float32
BF16 = jnp.bfloat16

GZ = 16
STEPS = 5
SMOOTHING = 0.25
COUPLING = 0.5

ROWS = 1024
CELLS = 2048
CHUNK = 128
CHUNKS = ROWS // CHUNK
DP = 8
MP = 16
MROWS = 9


def spread(tiles):
    parts = []
    for tile in tiles:
        high = tile.astype(BF16).astype(F32)
        low = tile - high
        for c in range(8):
            both = jnp.concatenate(
                [
                    jnp.broadcast_to(high[c : c + 1], (8, 128)),
                    jnp.broadcast_to(low[c : c + 1], (8, 128)),
                ],
                axis=0,
            )
            parts.append(both.astype(BF16))
    return jnp.concatenate(parts, axis=1)


def gathered(product, first):
    total = product[:8] + product[8:]
    sub = lax.broadcasted_iota(jnp.int32, (8, 128), 0)
    tile = jnp.zeros((8, 128), F32)
    for c in range(8):
        at = (first + c) * 128
        tile = jnp.where(sub == c, total[:, at : at + 128], tile)
    return tile


def regular(u, below, above, weight):
    lane = lax.broadcasted_iota(jnp.int32, (8, 128), 1)
    sub = lax.broadcasted_iota(jnp.int32, (8, 128), 0)
    outs = []
    for layer in range(2):
        for field in range(2):
            v = u[layer * 2 + field]
            beside = u[(1 - layer) * 2 + field] + (below[field] if layer == 0 else above[field])
            beside += jnp.where(lane % GZ != GZ - 1, pltpu.roll(v, 127, 1), 0.0)
            beside += jnp.where(lane % GZ != 0, pltpu.roll(v, 1, 1), 0.0)
            later = pltpu.roll(v, 128 - GZ, 1)
            wrapped = jnp.where(sub < 7, pltpu.roll(later, 7, 0), 0.0)
            beside += jnp.where(lane < 128 - GZ, later, wrapped)
            earlier = pltpu.roll(v, GZ, 1)
            wrapped = jnp.where(sub > 0, pltpu.roll(earlier, 1, 0), 0.0)
            beside += jnp.where(lane >= GZ, earlier, wrapped)
            other = u[layer * 2 + 1 - field]
            outs.append(weight[layer] * v + SMOOTHING * (6.0 * v - beside) + COUPLING * (v - other))
    return jnp.stack(outs)


def lanes_of(cells):
    return jnp.sum(jnp.sum(cells, axis=0), axis=0, keepdims=True)


def two_sums(one, two):
    lane = lax.broadcasted_iota(jnp.int32, (1, 128), 1)
    return jnp.where(lane < 64, one + pltpu.roll(one, 64, 1), two + pltpu.roll(two, 64, 1))


def split_sums(row):
    lane = lax.broadcasted_iota(jnp.int32, (1, 128), 1)
    one = jnp.sum(jnp.where(lane < 64, row, 0.0), axis=1, keepdims=True)
    two = jnp.sum(jnp.where(lane < 64, 0.0, row), axis=1, keepdims=True)
    return one, two


def kernel(
    x_ref, obs_ref, rw_ref, model_ref, smooth_ref, active_ref,
    upd_ref, res_ref,
    raw, wide, md, mt, mbuf, dbuf, ubuf, halo, smbuf, sdbuf,
    free, weight, x_s, r_s, p_s, s_s, z_s, rs_s, rr_s, base, coef, fs_s, fr_s, scal,
    load_sem, m_send, m_recv, d_send, d_recv, h_send, h_recv, s_send, s_recv,
):
    dp = lax.axis_index("dp")
    mp = lax.axis_index("mp")
    gravity = dp < DP * 3 // 4

    loads = [
        pltpu.make_async_copy(
            x_ref.at[pl.ds(k * CHUNK * 16, CHUNK * 16)],
            raw.at[pl.ds(k * CHUNK * 16, CHUNK * 16)],
            load_sem.at[k],
        )
        for k in range(CHUNKS)
    ]
    for load in loads:
        load.start()

    m_peers = [{"dp": dp, "mp": lax.rem(mp + k, MP)} for k in range(1, MP)]
    d_peers = [{"dp": lax.rem(dp + k, DP), "mp": mp} for k in range(1, DP)]
    barrier = pltpu.get_barrier_semaphore()
    for peer in m_peers + d_peers:
        pl.semaphore_signal(barrier, inc=1, device_id=peer, device_id_type=MESH)

    for layer in range(2):
        weight[layer] = smooth_ref[pl.ds(layer, 8, stride=2), :]
        for field in range(2):
            at = pl.ds(field * 16 + layer, 8, stride=2)
            ubuf[0, layer * 2 + field] = model_ref[at, :]
            free[layer * 2 + field] = 1.0 - active_ref[at, :].astype(F32)
    for ref in (x_s, p_s, s_s, z_s, rs_s):
        ref[...] = jnp.zeros_like(ref)
    fs_s[...] = jnp.zeros_like(fs_s)

    def chosen(u):
        return [jnp.where(gravity, u[layer * 2], u[layer * 2 + 1]) for layer in range(2)]

    left = spread(chosen(ubuf[0]))
    for k in range(CHUNKS):
        loads[k].wait()
        wide[...] = raw[pl.ds(k * CHUNK * 16, CHUNK * 16), :].astype(F32)
        for c in range(8):
            for layer in range(2):
                at = (layer * 8 + c) * 128
                part = wide[pl.ds(c * 2 + layer, CHUNK, stride=16), :]
                md[pl.ds(k * CHUNK, CHUNK), at : at + 128] = part.astype(BF16)
        some = lax.dot_general(
            left, md[pl.ds(k * CHUNK, CHUNK), :], (((1,), (1,)), ((), ())), preferred_element_type=F32
        )
        mbuf[0, mp, k : k + 1, :] = some[0:1] + some[8:9]
    mbuf[0, mp, 8:9, :] = jnp.zeros((1, 128), F32)

    pl.semaphore_wait(barrier, MP - 1 + DP - 1)

    def step(k, carry):
        now = lax.rem(k, 2)
        later = 1 - now

        mine = mbuf.at[now, mp, pl.ds(0, MROWS)]
        for peer in m_peers:
            pltpu.make_async_remote_copy(
                src_ref=mine, dst_ref=mine, send_sem=m_send.at[now], recv_sem=m_recv.at[now],
                device_id=peer, device_id_type=MESH,
            ).start()
        halo_copies = []
        for side, (first, peer) in enumerate(
            [(2, {"dp": dp, "mp": lax.rem(mp + 1, MP)}), (0, {"dp": dp, "mp": lax.rem(mp + MP - 1, MP)})]
        ):
            copy = pltpu.make_async_remote_copy(
                src_ref=ubuf.at[now, pl.ds(first, 2)], dst_ref=halo.at[now, side],
                send_sem=h_send.at[side], recv_sem=h_recv.at[now, side],
                device_id=peer, device_id_type=MESH,
            )
            copy.start()
            halo_copies.append(copy)

        @pl.when(k == 0)
        def _():
            row = lax.broadcasted_iota(jnp.int32, (256, 256), 0)
            col = lax.broadcasted_iota(jnp.int32, (256, 256), 1)
            eye = jnp.where(row == col, 1.0, 0.0).astype(BF16)

            def turn(j, carry):
                at = pl.multiple_of(j * 256, 256)
                turned = lax.dot_general(
                    eye, md[:, pl.ds(at, 256)], (((1,), (1,)), ((), ())), preferred_element_type=F32
                )
                mt[pl.ds(at, 256), :] = turned.astype(BF16)
                return carry

            lax.fori_loop(0, CELLS // 256, turn, 0)

        all_m = mbuf.at[now, pl.ds(0, MP - 1), pl.ds(0, MROWS)]
        pltpu.make_async_copy(all_m, all_m, m_recv.at[now]).wait()
        rows = mbuf[now, 0, 0:8]
        sums = mbuf[now, 0, 8:9]
        for j in range(1, MP):
            rows += mbuf[now, j, 0:8]
            sums += mbuf[now, j, 8:9]

        scaled = rw_ref[...] * (rows - jnp.where(k == 0, obs_ref[...], 0.0))
        product = jnp.dot(spread([scaled]), md[...], preferred_element_type=F32)
        dbuf[now, dp, 0:8] = gathered(product, 0)
        dbuf[now, dp, 8:16] = gathered(product, 8)
        mine_d = dbuf.at[now, dp]
        for peer in d_peers:
            pltpu.make_async_remote_copy(
                src_ref=mine_d, dst_ref=mine_d, send_sem=d_send.at[now], recv_sem=d_recv.at[now],
                device_id=peer, device_id_type=MESH,
            ).start()

        for copy in halo_copies:
            copy.wait()
        u = ubuf[now]
        below = jnp.where(mp > 0, halo[now, 0], 0.0)
        above = jnp.where(mp < MP - 1, halo[now, 1], 0.0)
        smooth = regular(u, below, above, weight[...])
        mask = free[...]

        @pl.when(k == 0)
        def _():
            base[...] = -(mask * smooth)
            coef[...] = -mask

        @pl.when(k == 1)
        def _():
            r_s[...] = u
            fr_s[...] = rows
            rr_s[...] = smooth
            base[...] = mask * smooth
            coef[...] = mask

        @pl.when(k >= 2)
        def _():
            gamma, delta = split_sums(sums)
            first = k == 2
            beta = jnp.where(first, 0.0, gamma / jnp.where(first, 1.0, scal[0, 0:1, 0:1]))
            past = beta * gamma / jnp.where(first, 1.0, scal[1, 0:1, 0:1])
            alpha = gamma / (delta - past)
            scal[0] = jnp.broadcast_to(gamma, (8, 128))
            scal[1] = jnp.broadcast_to(alpha, (8, 128))
            r = r_s[...]
            p = r + beta * p_s[...]
            s = u + beta * s_s[...]
            r = r - alpha * s
            p_s[...] = p
            s_s[...] = s
            r_s[...] = r
            x_s[...] = x_s[...] + alpha * p
            fs = rows + beta * fs_s[...]
            fr = fr_s[...] - alpha * fs
            fs_s[...] = fs
            fr_s[...] = fr
            rs = smooth + beta * rs_s[...]
            rr = rr_s[...] - alpha * rs
            rs_s[...] = rs
            rr_s[...] = rr
            zb = mask * smooth + beta * z_s[...]
            z_s[...] = zb
            base[...] = u - alpha * zb
            coef[...] = -(alpha * mask)

            @pl.when(k == STEPS - 1)
            def _():
                smbuf[mp] = jnp.broadcast_to(two_sums(lanes_of(r * r), lanes_of(r * rr)), (8, 128))
                sdbuf[dp] = rw_ref[...] * fr * fr
                for peer in m_peers:
                    pltpu.make_async_remote_copy(
                        src_ref=smbuf.at[mp], dst_ref=smbuf.at[mp], send_sem=s_send.at[0], recv_sem=s_recv.at[0],
                        device_id=peer, device_id_type=MESH,
                    ).start()
                for peer in d_peers:
                    pltpu.make_async_remote_copy(
                        src_ref=sdbuf.at[dp], dst_ref=sdbuf.at[dp], send_sem=s_send.at[1], recv_sem=s_recv.at[1],
                        device_id=peer, device_id_type=MESH,
                    ).start()

        pltpu.make_async_copy(all_m, all_m, m_send.at[now]).wait()
        all_d = dbuf.at[now, pl.ds(0, DP - 1)]
        pltpu.make_async_copy(all_d, all_d, d_recv.at[now]).wait()
        density = dbuf[now, 0]
        for j in range(1, 6):
            density += dbuf[now, j]
        suscept = dbuf[now, 6] + dbuf[now, 7]
        summed = jnp.stack([density[:8], suscept[:8], density[8:], suscept[8:]])
        v = base[...] + coef[...] * summed
        ubuf[later] = v
        z_s[...] = z_s[...] + jnp.where(k >= 2, mask, 0.0) * summed

        @pl.when(k < STEPS - 1)
        def _():
            product = jnp.dot(spread(chosen(v)), mt[...], preferred_element_type=F32)
            mbuf[later, mp, 0:8] = gathered(product, 0)
            r = r_s[...]
            mbuf[later, mp, 8:9] = two_sums(lanes_of(r * r), lanes_of(r * v))

        pltpu.make_async_copy(all_d, all_d, d_send.at[now]).wait()
        return carry

    r_s[...] = jnp.zeros_like(r_s)
    lax.fori_loop(0, STEPS, step, 0)

    all_sm = smbuf.at[pl.ds(0, MP - 1)]
    pltpu.make_async_copy(all_sm, all_sm, s_recv.at[0]).wait()
    all_sd = sdbuf.at[pl.ds(0, DP - 1)]
    pltpu.make_async_copy(all_sd, all_sd, s_recv.at[1]).wait()
    sums = smbuf[0]
    for j in range(1, MP):
        sums += smbuf[j]
    energy = sdbuf[0]
    for j in range(1, DP):
        energy += sdbuf[j]
    gamma, smoothed = split_sums(sums[0:1])
    delta = smoothed + jnp.sum(jnp.sum(energy, axis=0, keepdims=True), axis=1, keepdims=True)
    beta = gamma / scal[0, 0:1, 0:1]
    alpha = gamma / (delta - beta * gamma / scal[1, 0:1, 0:1])
    r = r_s[...]
    upd = x_s[...] + alpha * (r + beta * p_s[...])
    res = r - alpha * (ubuf[STEPS % 2] + beta * s_s[...])
    for layer in range(2):
        for field in range(2):
            at = pl.ds(field * 16 + layer, 8, stride=2)
            upd_ref[at, :] = upd[layer * 2 + field]
            res_ref[at, :] = res[layer * 2 + field]
    pltpu.make_async_copy(all_sm, all_sm, s_send.at[0]).wait()
    pltpu.make_async_copy(all_sd, all_sd, s_send.at[1]).wait()


def pairs(field):
    lead = field.shape[:-2]
    n = len(lead)
    cut = field.reshape(*lead, 2, 8, 128)
    return jnp.swapaxes(cut, n, n + 1).reshape(-1, 128)


def unpairs(rows):
    return jnp.swapaxes(rows.reshape(2, 8, 2, 128), 1, 2).reshape(2, 2, 1024)


def local(sensitivity, observed, row_weight, model, smooth_weight, active):
    vmem = pl.BlockSpec(memory_space=pltpu.VMEM)
    cells = pltpu.VMEM((4, 8, 128), F32)
    tile = pltpu.VMEM((8, 128), F32)
    upd, res = pl.pallas_call(
        kernel,
        out_shape=[jax.ShapeDtypeStruct((32, 128), F32)] * 2,
        in_specs=[pl.BlockSpec(memory_space=pl.ANY)] + [vmem] * 5,
        out_specs=[vmem, vmem],
        scratch_shapes=[
            pltpu.VMEM((ROWS * 16, 128), BF16),
            pltpu.VMEM((CHUNK * 16, 128), F32),
            pltpu.VMEM((ROWS, CELLS), BF16),
            pltpu.VMEM((CELLS, ROWS), BF16),
            pltpu.VMEM((2, MP, 16, 128), F32),
            pltpu.VMEM((2, DP, 16, 128), F32),
            pltpu.VMEM((2, 4, 8, 128), F32),
            pltpu.VMEM((2, 2, 2, 8, 128), F32),
            pltpu.VMEM((MP, 8, 128), F32),
            pltpu.VMEM((DP, 8, 128), F32),
            cells,
            pltpu.VMEM((2, 8, 128), F32),
            cells, cells, cells, cells, cells, cells, cells, cells, cells,
            tile, tile,
            pltpu.VMEM((2, 8, 128), F32),
            pltpu.SemaphoreType.DMA((CHUNKS,)),
            pltpu.SemaphoreType.DMA((2,)),
            pltpu.SemaphoreType.DMA((2,)),
            pltpu.SemaphoreType.DMA((2,)),
            pltpu.SemaphoreType.DMA((2,)),
            pltpu.SemaphoreType.DMA((2,)),
            pltpu.SemaphoreType.DMA((2, 2)),
            pltpu.SemaphoreType.DMA((2,)),
            pltpu.SemaphoreType.DMA((2,)),
        ],
        compiler_params=pltpu.CompilerParams(
            collective_id=0, has_side_effects=True, vmem_limit_bytes=32 * 2**20
        ),
    )(
        pairs(sensitivity),
        observed.reshape(8, 128),
        row_weight.reshape(8, 128),
        pairs(model),
        pairs(smooth_weight),
        pairs(active),
    )
    return unpairs(upd), unpairs(res)


def solution(mesh):
    return jax.shard_map(
        local,
        mesh=mesh,
        in_specs=(
            P("dp", "mp", None),
            P("dp"),
            P("dp"),
            P(None, "mp", None),
            P("mp", None),
            P(None, "mp", None),
        ),
        out_specs=(P(None, "mp", None), P(None, "mp", None)),
        check_vma=False,
    )
```

```python
import functools

import jax
import jax.numpy as jnp
from jax import lax
from jax.experimental import pallas as pl
from jax.experimental.pallas import tpu as pltpu
from jax.sharding import PartitionSpec as P

MESH = pl.DeviceIdType.MESH
F32 = jnp.float32
BF16 = jnp.bfloat16

GZ = 16
STEPS = 5
SMOOTHING = 0.25
COUPLING = 0.5

ROWS = 1024
CELLS = 2048
CHUNK = 128
CHUNKS = ROWS // CHUNK
DP = 8
MP = 16
MROWS = 9


def far_first(me, outer, inner, place):
    high, low = me // inner, lax.rem(me, inner)
    steps = [(a, b) for a in range(outer) for b in range(inner) if a or b]
    steps.sort(key=lambda s: -(min(s[0], outer - s[0]) + min(s[1], inner - s[1])))
    return [place(lax.rem(high + a, outer) * inner + lax.rem(low + b, inner)) for a, b in steps]


def spread(tiles):
    parts = []
    for tile in tiles:
        high = tile.astype(BF16).astype(F32)
        low = tile - high
        for c in range(8):
            both = jnp.concatenate(
                [
                    jnp.broadcast_to(high[c : c + 1], (8, 128)),
                    jnp.broadcast_to(low[c : c + 1], (8, 128)),
                ],
                axis=0,
            )
            parts.append(both.astype(BF16))
    return jnp.concatenate(parts, axis=1)


def gathered(product, first):
    total = product[:8] + product[8:]
    sub = lax.broadcasted_iota(jnp.int32, (8, 128), 0)
    tile = jnp.zeros((8, 128), F32)
    for c in range(8):
        at = (first + c) * 128
        tile = jnp.where(sub == c, total[:, at : at + 128], tile)
    return tile


def regular(u, below, above, weight):
    lane = lax.broadcasted_iota(jnp.int32, (8, 128), 1)
    sub = lax.broadcasted_iota(jnp.int32, (8, 128), 0)
    outs = []
    for layer in range(2):
        for field in range(2):
            v = u[layer * 2 + field]
            beside = u[(1 - layer) * 2 + field] + (below[field] if layer == 0 else above[field])
            beside += jnp.where(lane % GZ != GZ - 1, pltpu.roll(v, 127, 1), 0.0)
            beside += jnp.where(lane % GZ != 0, pltpu.roll(v, 1, 1), 0.0)
            later = pltpu.roll(v, 128 - GZ, 1)
            wrapped = jnp.where(sub < 7, pltpu.roll(later, 7, 0), 0.0)
            beside += jnp.where(lane < 128 - GZ, later, wrapped)
            earlier = pltpu.roll(v, GZ, 1)
            wrapped = jnp.where(sub > 0, pltpu.roll(earlier, 1, 0), 0.0)
            beside += jnp.where(lane >= GZ, earlier, wrapped)
            other = u[layer * 2 + 1 - field]
            outs.append(weight[layer] * v + SMOOTHING * (6.0 * v - beside) + COUPLING * (v - other))
    return jnp.stack(outs)


def lanes_of(cells):
    return jnp.sum(jnp.sum(cells, axis=0), axis=0, keepdims=True)


def two_sums(one, two):
    lane = lax.broadcasted_iota(jnp.int32, (1, 128), 1)
    return jnp.where(lane < 64, one + pltpu.roll(one, 64, 1), two + pltpu.roll(two, 64, 1))


def split_sums(row):
    lane = lax.broadcasted_iota(jnp.int32, (1, 128), 1)
    one = jnp.sum(jnp.where(lane < 64, row, 0.0), axis=1, keepdims=True)
    two = jnp.sum(jnp.where(lane < 64, 0.0, row), axis=1, keepdims=True)
    return one, two


def kernel(
    x_ref, obs_hbm, rw_hbm, model_hbm, smooth_hbm, active_hbm,
    out_ref,
    obs_ref, rw_ref, model_ref, smooth_ref, active_ref, raw, wide, md, mt, mbuf, dbuf, ubuf, halo, smbuf, sdbuf,
    free, weight, x_s, r_s, p_s, s_s, z_s, rs_s, rr_s, base, coef, fs_s, fr_s, scal,
    small_sem, load_sem, m_send, m_recv, d_send, d_recv, h_send, h_recv, s_send, s_recv,
):
    dp = lax.axis_index("dp")
    mp = lax.axis_index("mp")
    gravity = dp < DP * 3 // 4

    smalls = [
        pltpu.make_async_copy(src, dst, small_sem.at[k])
        for k, (src, dst) in enumerate(
            [
                (model_hbm, model_ref),
                (active_hbm, active_ref),
                (smooth_hbm, smooth_ref),
                (obs_hbm, obs_ref),
                (rw_hbm, rw_ref),
            ]
        )
    ]
    smalls[0].start()
    loads = [
        pltpu.make_async_copy(
            x_ref.at[pl.ds(k * CHUNK * 16, CHUNK * 16)],
            raw.at[pl.ds(k * CHUNK * 16, CHUNK * 16)],
            load_sem.at[k],
        )
        for k in range(CHUNKS)
    ]
    for load in loads:
        load.start()
    for small in smalls[1:]:
        small.start()

    m_peers = far_first(mp, MP // 4, 4, lambda other: {"dp": dp, "mp": other})
    d_peers = far_first(dp, 4, DP // 4, lambda other: {"dp": other, "mp": mp})
    barrier = pltpu.get_barrier_semaphore()
    for peer in m_peers + d_peers:
        pl.semaphore_signal(barrier, inc=1, device_id=peer, device_id_type=MESH)

    smalls[0].wait()
    for layer in range(2):
        for field in range(2):
            at = pl.ds(field * 16 + layer, 8, stride=2)
            ubuf[0, layer * 2 + field] = model_ref[at, :]
    for ref in (x_s, p_s, s_s, z_s, rs_s):
        ref[...] = jnp.zeros_like(ref)
    fs_s[...] = jnp.zeros_like(fs_s)

    def chosen(u):
        return [jnp.where(gravity, u[layer * 2], u[layer * 2 + 1]) for layer in range(2)]

    left = spread(chosen(ubuf[0]))
    for k in range(CHUNKS):
        loads[k].wait()
        wide[...] = raw[pl.ds(k * CHUNK * 16, CHUNK * 16), :].astype(F32)
        for c in range(8):
            for layer in range(2):
                at = (layer * 8 + c) * 128
                part = wide[pl.ds(c * 2 + layer, CHUNK, stride=16), :]
                md[pl.ds(k * CHUNK, CHUNK), at : at + 128] = part.astype(BF16)
        some = lax.dot_general(
            left, md[pl.ds(k * CHUNK, CHUNK), :], (((1,), (1,)), ((), ())), preferred_element_type=F32
        )
        mbuf[0, mp, k : k + 1, :] = some[0:1] + some[8:9]
    mbuf[0, mp, 8:9, :] = jnp.zeros((1, 128), F32)

    pl.semaphore_wait(barrier, MP - 1 + DP - 1)

    def step(k, carry):
        now = lax.rem(k, 2)
        later = 1 - now

        mine = mbuf.at[now, mp, pl.ds(0, MROWS)]
        for peer in m_peers:
            pltpu.make_async_remote_copy(
                src_ref=mine, dst_ref=mine, send_sem=m_send.at[now], recv_sem=m_recv.at[now],
                device_id=peer, device_id_type=MESH,
            ).start()
        halo_copies = []
        for side, (first, peer) in enumerate(
            [(2, {"dp": dp, "mp": lax.rem(mp + 1, MP)}), (0, {"dp": dp, "mp": lax.rem(mp + MP - 1, MP)})]
        ):
            copy = pltpu.make_async_remote_copy(
                src_ref=ubuf.at[now, pl.ds(first, 2)], dst_ref=halo.at[now, side],
                send_sem=h_send.at[side], recv_sem=h_recv.at[now, side],
                device_id=peer, device_id_type=MESH,
            )
            copy.start()
            halo_copies.append(copy)

        @pl.when(k == 0)
        def _():
            row = lax.broadcasted_iota(jnp.int32, (256, 256), 0)
            col = lax.broadcasted_iota(jnp.int32, (256, 256), 1)
            eye = jnp.where(row == col, 1.0, 0.0).astype(BF16)

            def turn(j, carry):
                at = pl.multiple_of(j * 256, 256)
                turned = lax.dot_general(
                    eye, md[:, pl.ds(at, 256)], (((1,), (1,)), ((), ())), preferred_element_type=F32
                )
                mt[pl.ds(at, 256), :] = turned.astype(BF16)
                return carry

            lax.fori_loop(0, CELLS // 256, turn, 0)
            for small in smalls[1:]:
                small.wait()
            for layer in range(2):
                weight[layer] = smooth_ref[pl.ds(layer, 8, stride=2), :]
                for field in range(2):
                    at = pl.ds(field * 16 + layer, 8, stride=2)
                    free[layer * 2 + field] = 1.0 - active_ref[at, :].astype(F32)

        all_m = mbuf.at[now, pl.ds(0, MP - 1), pl.ds(0, MROWS)]
        pltpu.make_async_copy(all_m, all_m, m_recv.at[now]).wait()
        rows = mbuf[now, 0, 0:8]
        sums = mbuf[now, 0, 8:9]
        for j in range(1, MP):
            rows += mbuf[now, j, 0:8]
            sums += mbuf[now, j, 8:9]

        scaled = rw_ref[...] * (rows - jnp.where(k == 0, obs_ref[...], 0.0))
        product = jnp.dot(spread([scaled]), md[...], preferred_element_type=F32)
        dbuf[now, dp, 0:8] = gathered(product, 0)
        dbuf[now, dp, 8:16] = gathered(product, 8)
        mine_d = dbuf.at[now, dp]
        for peer in d_peers:
            pltpu.make_async_remote_copy(
                src_ref=mine_d, dst_ref=mine_d, send_sem=d_send.at[now], recv_sem=d_recv.at[now],
                device_id=peer, device_id_type=MESH,
            ).start()

        for copy in halo_copies:
            copy.wait()
        u = ubuf[now]
        below = jnp.where(mp > 0, halo[now, 0], 0.0)
        above = jnp.where(mp < MP - 1, halo[now, 1], 0.0)
        smooth = regular(u, below, above, weight[...])
        mask = free[...]

        @pl.when(k == 0)
        def _():
            base[...] = -(mask * smooth)
            coef[...] = -mask

        @pl.when(k == 1)
        def _():
            r_s[...] = u
            fr_s[...] = rows
            rr_s[...] = smooth
            base[...] = mask * smooth
            coef[...] = mask

        @pl.when(k >= 2)
        def _():
            gamma, delta = split_sums(sums)
            first = k == 2
            beta = jnp.where(first, 0.0, gamma / jnp.where(first, 1.0, scal[0, 0:1, 0:1]))
            past = beta * gamma / jnp.where(first, 1.0, scal[1, 0:1, 0:1])
            alpha = gamma / (delta - past)
            scal[0] = jnp.broadcast_to(gamma, (8, 128))
            scal[1] = jnp.broadcast_to(alpha, (8, 128))
            r = r_s[...]
            p = r + beta * p_s[...]
            s = u + beta * s_s[...]
            r = r - alpha * s
            p_s[...] = p
            s_s[...] = s
            r_s[...] = r
            x_s[...] = x_s[...] + alpha * p
            fs = rows + beta * fs_s[...]
            fr = fr_s[...] - alpha * fs
            fs_s[...] = fs
            fr_s[...] = fr
            rs = smooth + beta * rs_s[...]
            rr = rr_s[...] - alpha * rs
            rs_s[...] = rs
            rr_s[...] = rr
            zb = mask * smooth + beta * z_s[...]
            z_s[...] = zb
            base[...] = u - alpha * zb
            coef[...] = -(alpha * mask)

            @pl.when(k == STEPS - 1)
            def _():
                smbuf[mp] = jnp.broadcast_to(two_sums(lanes_of(r * r), lanes_of(r * rr)), (8, 128))
                sdbuf[dp] = rw_ref[...] * fr * fr
                for peer in m_peers:
                    pltpu.make_async_remote_copy(
                        src_ref=smbuf.at[mp], dst_ref=smbuf.at[mp], send_sem=s_send.at[0], recv_sem=s_recv.at[0],
                        device_id=peer, device_id_type=MESH,
                    ).start()
                for peer in d_peers:
                    pltpu.make_async_remote_copy(
                        src_ref=sdbuf.at[dp], dst_ref=sdbuf.at[dp], send_sem=s_send.at[1], recv_sem=s_recv.at[1],
                        device_id=peer, device_id_type=MESH,
                    ).start()

        pltpu.make_async_copy(all_m, all_m, m_send.at[now]).wait()
        all_d = dbuf.at[now, pl.ds(0, DP - 1)]
        pltpu.make_async_copy(all_d, all_d, d_recv.at[now]).wait()
        density = dbuf[now, 0]
        for j in range(1, 6):
            density += dbuf[now, j]
        suscept = dbuf[now, 6] + dbuf[now, 7]
        summed = jnp.stack([density[:8], suscept[:8], density[8:], suscept[8:]])
        v = base[...] + coef[...] * summed
        ubuf[later] = v
        z_s[...] = z_s[...] + jnp.where(k >= 2, mask, 0.0) * summed

        @pl.when(k < STEPS - 1)
        def _():
            product = jnp.dot(spread(chosen(v)), mt[...], preferred_element_type=F32)
            mbuf[later, mp, 0:8] = gathered(product, 0)
            r = r_s[...]
            mbuf[later, mp, 8:9] = two_sums(lanes_of(r * r), lanes_of(r * v))

        pltpu.make_async_copy(all_d, all_d, d_send.at[now]).wait()
        return carry

    r_s[...] = jnp.zeros_like(r_s)
    lax.fori_loop(0, STEPS, step, 0)

    all_sm = smbuf.at[pl.ds(0, MP - 1)]
    pltpu.make_async_copy(all_sm, all_sm, s_recv.at[0]).wait()
    all_sd = sdbuf.at[pl.ds(0, DP - 1)]
    pltpu.make_async_copy(all_sd, all_sd, s_recv.at[1]).wait()
    sums = smbuf[0]
    for j in range(1, MP):
        sums += smbuf[j]
    energy = sdbuf[0]
    for j in range(1, DP):
        energy += sdbuf[j]
    gamma, smoothed = split_sums(sums[0:1])
    delta = smoothed + jnp.sum(jnp.sum(energy, axis=0, keepdims=True), axis=1, keepdims=True)
    beta = gamma / scal[0, 0:1, 0:1]
    alpha = gamma / (delta - beta * gamma / scal[1, 0:1, 0:1])
    r = r_s[...]
    upd = x_s[...] + alpha * (r + beta * p_s[...])
    res = r - alpha * (ubuf[STEPS % 2] + beta * s_s[...])
    for layer in range(2):
        for field in range(2):
            at = pl.ds(field * 16 + layer, 8, stride=2)
            out_ref[0, at, :] = upd[layer * 2 + field]
            out_ref[1, at, :] = res[layer * 2 + field]
    pltpu.make_async_copy(all_sm, all_sm, s_send.at[0]).wait()
    pltpu.make_async_copy(all_sd, all_sd, s_send.at[1]).wait()


def pairs(field):
    lead = field.shape[:-2]
    n = len(lead)
    cut = field.reshape(*lead, 2, 8, 128)
    return jnp.swapaxes(cut, n, n + 1).reshape(-1, 128)


def unpairs(rows):
    return jnp.swapaxes(rows.reshape(2, 2, 8, 2, 128), 2, 3).reshape(2, 2, 2, 1024)


def local(sensitivity, observed, row_weight, model, smooth_weight, active):
    vmem = pl.BlockSpec(memory_space=pltpu.VMEM)
    cells = pltpu.VMEM((4, 8, 128), F32)
    tile = pltpu.VMEM((8, 128), F32)
    out = pl.pallas_call(
        kernel,
        out_shape=jax.ShapeDtypeStruct((2, 32, 128), F32),
        in_specs=[pl.BlockSpec(memory_space=pltpu.HBM)] * 6,
        out_specs=vmem,
        scratch_shapes=[
            tile, tile,
            pltpu.VMEM((32, 128), F32),
            pltpu.VMEM((16, 128), F32),
            pltpu.VMEM((32, 128), jnp.int32),
            pltpu.VMEM((ROWS * 16, 128), BF16),
            pltpu.VMEM((CHUNK * 16, 128), F32),
            pltpu.VMEM((ROWS, CELLS), BF16),
            pltpu.VMEM((CELLS, ROWS), BF16),
            pltpu.VMEM((2, MP, 16, 128), F32),
            pltpu.VMEM((2, DP, 16, 128), F32),
            pltpu.VMEM((2, 4, 8, 128), F32),
            pltpu.VMEM((2, 2, 2, 8, 128), F32),
            pltpu.VMEM((MP, 8, 128), F32),
            pltpu.VMEM((DP, 8, 128), F32),
            cells,
            pltpu.VMEM((2, 8, 128), F32),
            cells, cells, cells, cells, cells, cells, cells, cells, cells,
            tile, tile,
            pltpu.VMEM((2, 8, 128), F32),
            pltpu.SemaphoreType.DMA((5,)),
            pltpu.SemaphoreType.DMA((CHUNKS,)),
            pltpu.SemaphoreType.DMA((2,)),
            pltpu.SemaphoreType.DMA((2,)),
            pltpu.SemaphoreType.DMA((2,)),
            pltpu.SemaphoreType.DMA((2,)),
            pltpu.SemaphoreType.DMA((2,)),
            pltpu.SemaphoreType.DMA((2, 2)),
            pltpu.SemaphoreType.DMA((2,)),
            pltpu.SemaphoreType.DMA((2,)),
        ],
        compiler_params=pltpu.CompilerParams(
            collective_id=0, has_side_effects=True, vmem_limit_bytes=60 * 2**20
        ),
    )(
        pairs(sensitivity),
        observed.reshape(8, 128),
        row_weight.reshape(8, 128),
        pairs(model),
        pairs(smooth_weight),
        pairs(active),
    )
    both = unpairs(out)
    return both[0], both[1]


def solution(mesh):
    return jax.shard_map(
        local,
        mesh=mesh,
        in_specs=(
            P("dp", "mp", None),
            P("dp"),
            P("dp"),
            P(None, "mp", None),
            P("mp", None),
            P(None, "mp", None),
        ),
        out_specs=(P(None, "mp", None), P(None, "mp", None)),
        check_vma=False,
    )
```

```python
import functools

import jax
import jax.numpy as jnp
from jax import lax
from jax.experimental import pallas as pl
from jax.experimental.pallas import tpu as pltpu
from jax.sharding import PartitionSpec as P

MESH = pl.DeviceIdType.MESH
F32 = jnp.float32
BF16 = jnp.bfloat16

GZ = 16
STEPS = 5
SMOOTHING = 0.25
COUPLING = 0.5

ROWS = 1024
CELLS = 2048
CHUNK = 64
CHUNKS = ROWS // CHUNK
DP = 8
MP = 16
MROWS = 9
SROWS = 12


def far_first(me, outer, inner, place):
    high, low = me // inner, lax.rem(me, inner)
    steps = [(a, b) for a in range(outer) for b in range(inner) if a or b]
    steps.sort(key=lambda s: -(min(s[0], outer - s[0]) + min(s[1], inner - s[1])))
    return [place(lax.rem(high + a, outer) * inner + lax.rem(low + b, inner)) for a, b in steps]


def spread(tiles):
    parts = []
    for tile in tiles:
        high = tile.astype(BF16).astype(F32)
        low = tile - high
        for c in range(8):
            both = jnp.concatenate(
                [
                    jnp.broadcast_to(high[c : c + 1], (8, 128)),
                    jnp.broadcast_to(low[c : c + 1], (8, 128)),
                ],
                axis=0,
            )
            parts.append(both.astype(BF16))
    return jnp.concatenate(parts, axis=1)


def gathered(product, first):
    total = product[:8] + product[8:]
    sub = lax.broadcasted_iota(jnp.int32, (8, 128), 0)
    tile = jnp.zeros((8, 128), F32)
    for c in range(8):
        at = (first + c) * 128
        tile = jnp.where(sub == c, total[:, at : at + 128], tile)
    return tile


def regular(u, below, above, weight):
    lane = lax.broadcasted_iota(jnp.int32, (8, 128), 1)
    sub = lax.broadcasted_iota(jnp.int32, (8, 128), 0)
    outs = []
    for layer in range(2):
        for field in range(2):
            v = u[layer * 2 + field]
            beside = u[(1 - layer) * 2 + field] + (below[field] if layer == 0 else above[field])
            beside += jnp.where(lane % GZ != GZ - 1, pltpu.roll(v, 127, 1), 0.0)
            beside += jnp.where(lane % GZ != 0, pltpu.roll(v, 1, 1), 0.0)
            later = pltpu.roll(v, 128 - GZ, 1)
            wrapped = jnp.where(sub < 7, pltpu.roll(later, 7, 0), 0.0)
            beside += jnp.where(lane < 128 - GZ, later, wrapped)
            earlier = pltpu.roll(v, GZ, 1)
            wrapped = jnp.where(sub > 0, pltpu.roll(earlier, 1, 0), 0.0)
            beside += jnp.where(lane >= GZ, earlier, wrapped)
            other = u[layer * 2 + 1 - field]
            outs.append(weight[layer] * v + SMOOTHING * (6.0 * v - beside) + COUPLING * (v - other))
    return jnp.stack(outs)


def lanes_of(cells):
    return jnp.sum(jnp.sum(cells, axis=0), axis=0, keepdims=True)


def two_sums(one, two):
    lane = lax.broadcasted_iota(jnp.int32, (1, 128), 1)
    return jnp.where(lane < 64, one + pltpu.roll(one, 64, 1), two + pltpu.roll(two, 64, 1))


def split_sums(row):
    lane = lax.broadcasted_iota(jnp.int32, (1, 128), 1)
    one = jnp.sum(jnp.where(lane < 64, row, 0.0), axis=1, keepdims=True)
    two = jnp.sum(jnp.where(lane < 64, 0.0, row), axis=1, keepdims=True)
    return one, two


def kernel(
    x_ref, obs_hbm, rw_hbm, model_hbm, smooth_hbm, active_hbm,
    out_ref,
    obs_ref, rw_ref, model_ref, smooth_ref, active_ref, raw, halves, md, mt, mbuf, dbuf, ubuf, halo, smbuf, sdbuf,
    free, weight, x_s, r_s, p_s, s_s, z_s, rs_s, rr_s, base, coef, fs_s, fr_s, scal,
    small_sem, load_sem, m_send, m_recv, d_send, d_recv, h_send, h_recv, s_send, s_recv,
):
    dp = lax.axis_index("dp")
    mp = lax.axis_index("mp")
    gravity = dp < DP * 3 // 4

    smalls = [
        pltpu.make_async_copy(src, dst, small_sem.at[k])
        for k, (src, dst) in enumerate(
            [
                (model_hbm, model_ref),
                (active_hbm, active_ref),
                (smooth_hbm, smooth_ref),
                (obs_hbm, obs_ref),
                (rw_hbm, rw_ref),
            ]
        )
    ]
    smalls[0].start()
    loads = [
        pltpu.make_async_copy(
            x_ref.at[pl.ds(k * CHUNK * 16, CHUNK * 16)],
            raw.at[pl.ds(k * CHUNK * 16, CHUNK * 16)],
            load_sem.at[k],
        )
        for k in range(CHUNKS)
    ]
    for load in loads:
        load.start()
    for small in smalls[1:]:
        small.start()

    m_peers = far_first(mp, MP // 4, 4, lambda other: {"dp": dp, "mp": other})
    d_peers = far_first(dp, 4, DP // 4, lambda other: {"dp": other, "mp": mp})
    barrier = pltpu.get_barrier_semaphore()
    for peer in m_peers + d_peers:
        pl.semaphore_signal(barrier, inc=1, device_id=peer, device_id_type=MESH)

    smalls[0].wait()
    for layer in range(2):
        for field in range(2):
            at = pl.ds(field * 16 + layer, 8, stride=2)
            ubuf[0, layer * 2 + field] = model_ref[at, :]
    for ref in (x_s, p_s, s_s, z_s, rs_s):
        ref[...] = jnp.zeros_like(ref)
    fs_s[...] = jnp.zeros_like(fs_s)
    sdbuf[dp] = jnp.zeros((8, 128), F32)

    def chosen(u):
        return [jnp.where(gravity, u[layer * 2], u[layer * 2 + 1]) for layer in range(2)]

    first = chosen(ubuf[0])
    for k in range(CHUNKS):
        loads[k].wait()
        block = raw[pl.ds(k * CHUNK * 16, CHUNK * 16), :].reshape(CHUNK, 16, 128)
        turned = jnp.swapaxes(block, 0, 1)
        acc = jnp.zeros((CHUNK, 128), F32)
        for c in range(8):
            for layer in range(2):
                at = (layer * 8 + c) * 128
                part = turned[c * 2 + layer]
                md[pl.ds(k * CHUNK, CHUNK), at : at + 128] = part
                acc += part.astype(F32) * first[layer][c : c + 1]
        high = acc.astype(BF16)
        halves[pl.ds(k * CHUNK, CHUNK), :128] = high
        halves[pl.ds(k * CHUNK, CHUNK), 128:] = (acc - high.astype(F32)).astype(BF16)
    ones = jnp.ones((16, 256), BF16)
    sums = lax.dot_general(ones, halves[...], (((1,), (1,)), ((), ())), preferred_element_type=F32)
    for c in range(8):
        mbuf[0, mp, c : c + 1, :] = sums[0:1, c * 128 : c * 128 + 128]
    mbuf[0, mp, 8:9, :] = jnp.zeros((1, 128), F32)

    pl.semaphore_wait(barrier, MP - 1 + DP - 1)
    scalar_blocks = [smbuf.at[pl.ds(0, MP - 1), pl.ds(0, SROWS)], sdbuf.at[pl.ds(0, DP - 1)]]

    def step(k, carry):
        now = lax.rem(k, 2)
        later = 1 - now

        mine = mbuf.at[now, mp, pl.ds(0, MROWS)]
        for peer in m_peers:
            pltpu.make_async_remote_copy(
                src_ref=mine, dst_ref=mine, send_sem=m_send.at[now], recv_sem=m_recv.at[now],
                device_id=peer, device_id_type=MESH,
            ).start()
        halo_copies = []
        for side, (first, peer) in enumerate(
            [(2, {"dp": dp, "mp": lax.rem(mp + 1, MP)}), (0, {"dp": dp, "mp": lax.rem(mp + MP - 1, MP)})]
        ):
            copy = pltpu.make_async_remote_copy(
                src_ref=ubuf.at[now, pl.ds(first, 2)], dst_ref=halo.at[now, side],
                send_sem=h_send.at[side], recv_sem=h_recv.at[now, side],
                device_id=peer, device_id_type=MESH,
            )
            copy.start()
            halo_copies.append(copy)

        @pl.when(k == 0)
        def _():
            row = lax.broadcasted_iota(jnp.int32, (256, 256), 0)
            col = lax.broadcasted_iota(jnp.int32, (256, 256), 1)
            eye = jnp.where(row == col, 1.0, 0.0).astype(BF16)

            def turn(j, carry):
                at = pl.multiple_of(j * 256, 256)
                turned = lax.dot_general(
                    eye, md[:, pl.ds(at, 256)], (((1,), (1,)), ((), ())), preferred_element_type=F32
                )
                mt[pl.ds(at, 256), :] = turned.astype(BF16)
                return carry

            lax.fori_loop(0, CELLS // 256, turn, 0)
            for small in smalls[1:]:
                small.wait()
            for layer in range(2):
                weight[layer] = smooth_ref[pl.ds(layer, 8, stride=2), :]
                for field in range(2):
                    at = pl.ds(field * 16 + layer, 8, stride=2)
                    free[layer * 2 + field] = 1.0 - active_ref[at, :].astype(F32)

        for copy in halo_copies:
            copy.wait()
        u = ubuf[now]
        below = jnp.where(mp > 0, halo[now, 0], 0.0)
        above = jnp.where(mp < MP - 1, halo[now, 1], 0.0)
        smooth = regular(u, below, above, weight[...])
        mask = free[...]

        @pl.when(k == STEPS - 1)
        def _():
            r, s, rr, rs = r_s[...], s_s[...], rr_s[...], rs_s[...]
            pairs_of = [(r, r), (u, r), (s, r), (u, u), (u, s), (s, s), (r, rr), (u, rr), (s, rr), (u, smooth), (u, rs), (s, rs)]
            for j, (one, two) in enumerate(pairs_of):
                smbuf[mp, j : j + 1] = lanes_of(one * two)
            mine_s = smbuf.at[mp, pl.ds(0, SROWS)]
            for peer in m_peers:
                pltpu.make_async_remote_copy(
                    src_ref=mine_s, dst_ref=mine_s, send_sem=s_send.at[0], recv_sem=s_recv.at[0],
                    device_id=peer, device_id_type=MESH,
                ).start()

        all_m = mbuf.at[now, pl.ds(0, MP - 1), pl.ds(0, MROWS)]
        pltpu.make_async_copy(all_m, all_m, m_recv.at[now]).wait()
        rows = mbuf[now, 0, 0:8]
        sums = mbuf[now, 0, 8:9]
        for j in range(1, MP):
            rows += mbuf[now, j, 0:8]
            sums += mbuf[now, j, 8:9]

        scaled = rw_ref[...] * (rows - jnp.where(k == 0, obs_ref[...], 0.0))
        product = jnp.dot(spread([scaled]), md[...], preferred_element_type=F32)
        dbuf[now, dp, 0:8] = gathered(product, 0)
        dbuf[now, dp, 8:16] = gathered(product, 8)
        mine_d = dbuf.at[now, dp]
        for peer in d_peers:
            pltpu.make_async_remote_copy(
                src_ref=mine_d, dst_ref=mine_d, send_sem=d_send.at[now], recv_sem=d_recv.at[now],
                device_id=peer, device_id_type=MESH,
            ).start()

        @pl.when(k == STEPS - 1)
        def _():
            fr, fs = fr_s[...], fs_s[...]
            for j, (one, two) in enumerate([(fr, fr), (rows, fr), (fs, fr), (rows, rows), (rows, fs), (fs, fs)]):
                sdbuf[dp, j : j + 1] = jnp.sum(rw_ref[...] * one * two, axis=0, keepdims=True)
            mine_e = sdbuf.at[dp]
            for peer in d_peers:
                pltpu.make_async_remote_copy(
                    src_ref=mine_e, dst_ref=mine_e, send_sem=s_send.at[1], recv_sem=s_recv.at[1],
                    device_id=peer, device_id_type=MESH,
                ).start()

        @pl.when(k == 0)
        def _():
            base[...] = -(mask * smooth)
            coef[...] = -mask

        @pl.when(k == 1)
        def _():
            r_s[...] = u
            fr_s[...] = rows
            rr_s[...] = smooth
            base[...] = mask * smooth
            coef[...] = mask

        @pl.when(k >= 2)
        def _():
            gamma, delta = split_sums(sums)
            first = k == 2
            beta = jnp.where(first, 0.0, gamma / jnp.where(first, 1.0, scal[0, 0:1, 0:1]))
            past = beta * gamma / jnp.where(first, 1.0, scal[1, 0:1, 0:1])
            alpha = gamma / (delta - past)
            scal[0] = jnp.broadcast_to(gamma, (8, 128))
            scal[1] = jnp.broadcast_to(alpha, (8, 128))
            scal[2] = jnp.broadcast_to(beta, (8, 128))
            r = r_s[...]
            p = r + beta * p_s[...]
            s = u + beta * s_s[...]
            r = r - alpha * s
            p_s[...] = p
            s_s[...] = s
            r_s[...] = r
            x_s[...] = x_s[...] + alpha * p
            fs = rows + beta * fs_s[...]
            fr = fr_s[...] - alpha * fs
            fs_s[...] = fs
            fr_s[...] = fr
            rs = smooth + beta * rs_s[...]
            rr = rr_s[...] - alpha * rs
            rs_s[...] = rs
            rr_s[...] = rr
            zb = mask * smooth + beta * z_s[...]
            z_s[...] = zb
            base[...] = u - alpha * zb
            coef[...] = -(alpha * mask)

        @pl.when(k == STEPS - 1)
        def _():
            for n, others in enumerate(scalar_blocks):
                pltpu.make_async_copy(others, others, s_recv.at[n]).wait()
            dots = smbuf[0, 0:SROWS]
            for j in range(1, MP):
                dots += smbuf[j, 0:SROWS]
            weighed = sdbuf[0]
            for j in range(1, DP):
                weighed += sdbuf[j]
            a, b, g = scal[1, 0:1, 0:1], scal[2, 0:1, 0:1], scal[0, 0:1, 0:1]

            def after(rows):
                rr, wr, sr, ww, ws, ss = (rows[j : j + 1] for j in range(6))
                terms = rr - (2.0 * a) * (wr + b * sr) + (a * a) * (ww + (2.0 * b) * ws + (b * b) * ss)
                return jnp.sum(terms, axis=1, keepdims=True)

            gamma = after(dots[0:6])
            delta = after(dots[6:12]) + after(weighed[0:6])
            beta = gamma / g
            alpha = gamma / (delta - beta * gamma / a)
            r = r_s[...]
            upd = x_s[...] + alpha * (r + beta * p_s[...])
            base[...] = r - alpha * (beta * s_s[...] + base[...])
            coef[...] = -(alpha * coef[...])
            for layer in range(2):
                for field in range(2):
                    out_ref[0, pl.ds(field * 16 + layer, 8, stride=2), :] = upd[layer * 2 + field]

        pltpu.make_async_copy(all_m, all_m, m_send.at[now]).wait()
        all_d = dbuf.at[now, pl.ds(0, DP - 1)]
        pltpu.make_async_copy(all_d, all_d, d_recv.at[now]).wait()
        density = dbuf[now, 0]
        for j in range(1, 6):
            density += dbuf[now, j]
        suscept = dbuf[now, 6] + dbuf[now, 7]
        summed = jnp.stack([density[:8], suscept[:8], density[8:], suscept[8:]])
        v = base[...] + coef[...] * summed
        ubuf[later] = v
        z_s[...] = z_s[...] + jnp.where(k >= 2, mask, 0.0) * summed

        @pl.when(k < STEPS - 1)
        def _():
            product = jnp.dot(spread(chosen(v)), mt[...], preferred_element_type=F32)
            mbuf[later, mp, 0:8] = gathered(product, 0)
            r = r_s[...]
            mbuf[later, mp, 8:9] = two_sums(lanes_of(r * r), lanes_of(r * v))

        pltpu.make_async_copy(all_d, all_d, d_send.at[now]).wait()
        return carry

    r_s[...] = jnp.zeros_like(r_s)
    lax.fori_loop(0, STEPS, step, 0)

    res = ubuf[STEPS % 2]
    for layer in range(2):
        for field in range(2):
            out_ref[1, pl.ds(field * 16 + layer, 8, stride=2), :] = res[layer * 2 + field]
    for n, others in enumerate(scalar_blocks):
        pltpu.make_async_copy(others, others, s_send.at[n]).wait()


def pairs(field):
    lead = field.shape[:-2]
    n = len(lead)
    cut = field.reshape(*lead, 2, 8, 128)
    return jnp.swapaxes(cut, n, n + 1).reshape(-1, 128)


def unpairs(rows):
    return jnp.swapaxes(rows.reshape(2, 2, 8, 2, 128), 2, 3).reshape(2, 2, 2, 1024)


def local(sensitivity, observed, row_weight, model, smooth_weight, active):
    vmem = pl.BlockSpec(memory_space=pltpu.VMEM)
    cells = pltpu.VMEM((4, 8, 128), F32)
    tile = pltpu.VMEM((8, 128), F32)
    out = pl.pallas_call(
        kernel,
        out_shape=jax.ShapeDtypeStruct((2, 32, 128), F32),
        in_specs=[pl.BlockSpec(memory_space=pltpu.HBM)] * 6,
        out_specs=vmem,
        scratch_shapes=[
            tile, tile,
            pltpu.VMEM((32, 128), F32),
            pltpu.VMEM((16, 128), F32),
            pltpu.VMEM((32, 128), jnp.int32),
            pltpu.VMEM((ROWS * 16, 128), BF16),
            pltpu.VMEM((ROWS, 256), BF16),
            pltpu.VMEM((ROWS, CELLS), BF16),
            pltpu.VMEM((CELLS, ROWS), BF16),
            pltpu.VMEM((2, MP, 16, 128), F32),
            pltpu.VMEM((2, DP, 16, 128), F32),
            pltpu.VMEM((2, 4, 8, 128), F32),
            pltpu.VMEM((2, 2, 2, 8, 128), F32),
            pltpu.VMEM((MP, 16, 128), F32),
            pltpu.VMEM((DP, 8, 128), F32),
            cells,
            pltpu.VMEM((2, 8, 128), F32),
            cells, cells, cells, cells, cells, cells, cells, cells, cells,
            tile, tile,
            pltpu.VMEM((3, 8, 128), F32),
            pltpu.SemaphoreType.DMA((5,)),
            pltpu.SemaphoreType.DMA((CHUNKS,)),
            pltpu.SemaphoreType.DMA((2,)),
            pltpu.SemaphoreType.DMA((2,)),
            pltpu.SemaphoreType.DMA((2,)),
            pltpu.SemaphoreType.DMA((2,)),
            pltpu.SemaphoreType.DMA((2,)),
            pltpu.SemaphoreType.DMA((2, 2)),
            pltpu.SemaphoreType.DMA((2,)),
            pltpu.SemaphoreType.DMA((2,)),
        ],
        compiler_params=pltpu.CompilerParams(
            collective_id=0, has_side_effects=True, vmem_limit_bytes=60 * 2**20
        ),
    )(
        pairs(sensitivity),
        observed.reshape(8, 128),
        row_weight.reshape(8, 128),
        pairs(model),
        pairs(smooth_weight),
        pairs(active),
    )
    both = unpairs(out)
    return both[0], both[1]


def solution(mesh):
    return jax.shard_map(
        local,
        mesh=mesh,
        in_specs=(
            P("dp", "mp", None),
            P("dp"),
            P("dp"),
            P(None, "mp", None),
            P("mp", None),
            P(None, "mp", None),
        ),
        out_specs=(P(None, "mp", None), P(None, "mp", None)),
        check_vma=False,
    )
```

```python
import functools

import jax
import jax.numpy as jnp
from jax import lax
from jax.experimental import pallas as pl
from jax.experimental.pallas import tpu as pltpu
from jax.sharding import PartitionSpec as P

MESH = pl.DeviceIdType.MESH
F32 = jnp.float32
BF16 = jnp.bfloat16

GZ = 16
STEPS = 5
SMOOTHING = 0.25
COUPLING = 0.5

ROWS = 1024
CELLS = 2048
CHUNK = 64
CHUNKS = ROWS // CHUNK
DP = 8
MP = 16
MROWS = 9
SROWS = 12


def far_first(me, outer, inner, place):
    high, low = me // inner, lax.rem(me, inner)
    steps = [(a, b) for a in range(outer) for b in range(inner) if a or b]
    steps.sort(key=lambda s: -(min(s[0], outer - s[0]) + min(s[1], inner - s[1])))
    return [place(lax.rem(high + a, outer) * inner + lax.rem(low + b, inner)) for a, b in steps]


def spread(tiles):
    parts = []
    for tile in tiles:
        high = tile.astype(BF16).astype(F32)
        low = tile - high
        for c in range(8):
            both = jnp.concatenate(
                [
                    jnp.broadcast_to(high[c : c + 1], (8, 128)),
                    jnp.broadcast_to(low[c : c + 1], (8, 128)),
                ],
                axis=0,
            )
            parts.append(both.astype(BF16))
    return jnp.concatenate(parts, axis=1)


def product(tiles, matrix, split):
    width = matrix.shape[1]
    sums = [None] * ((width - split) // 128)
    for q in range(matrix.shape[0] // 128):
        row = tiles[q // 8][q % 8 : q % 8 + 1]
        column = jnp.transpose(jnp.broadcast_to(row, (128, 128)))
        for j in range(len(sums)):
            at = split + j * 128
            term = matrix[pl.ds(q * 128, 128), at : at + 128].astype(F32) * column
            term = jnp.sum(term.reshape(16, 8, 128), axis=0)
            sums[j] = term if sums[j] is None else sums[j] + term
    both = jnp.dot(spread(tiles), matrix[:, :split], preferred_element_type=F32)
    total = both[:8] + both[8:]
    outs = [total[:, at : at + 128] for at in range(0, split, 128)]
    return outs + [jnp.broadcast_to(jnp.sum(one, axis=0, keepdims=True), (8, 128)) for one in sums]


def gathered(outs):
    sub = lax.broadcasted_iota(jnp.int32, (8, 128), 0)
    tile = outs[0]
    for c in range(1, 8):
        tile = jnp.where(sub == c, outs[c], tile)
    return tile


def regular(u, below, above, weight):
    lane = lax.broadcasted_iota(jnp.int32, (8, 128), 1)
    sub = lax.broadcasted_iota(jnp.int32, (8, 128), 0)
    outs = []
    for layer in range(2):
        for field in range(2):
            v = u[layer * 2 + field]
            beside = u[(1 - layer) * 2 + field] + (below[field] if layer == 0 else above[field])
            beside += jnp.where(lane % GZ != GZ - 1, pltpu.roll(v, 127, 1), 0.0)
            beside += jnp.where(lane % GZ != 0, pltpu.roll(v, 1, 1), 0.0)
            later = pltpu.roll(v, 128 - GZ, 1)
            wrapped = jnp.where(sub < 7, pltpu.roll(later, 7, 0), 0.0)
            beside += jnp.where(lane < 128 - GZ, later, wrapped)
            earlier = pltpu.roll(v, GZ, 1)
            wrapped = jnp.where(sub > 0, pltpu.roll(earlier, 1, 0), 0.0)
            beside += jnp.where(lane >= GZ, earlier, wrapped)
            other = u[layer * 2 + 1 - field]
            outs.append(weight[layer] * v + SMOOTHING * (6.0 * v - beside) + COUPLING * (v - other))
    return jnp.stack(outs)


def lanes_of(cells):
    return jnp.sum(jnp.sum(cells, axis=0), axis=0, keepdims=True)


def two_sums(one, two):
    lane = lax.broadcasted_iota(jnp.int32, (1, 128), 1)
    return jnp.where(lane < 64, one + pltpu.roll(one, 64, 1), two + pltpu.roll(two, 64, 1))


def split_sums(row):
    lane = lax.broadcasted_iota(jnp.int32, (1, 128), 1)
    one = jnp.sum(jnp.where(lane < 64, row, 0.0), axis=1, keepdims=True)
    two = jnp.sum(jnp.where(lane < 64, 0.0, row), axis=1, keepdims=True)
    return one, two


def kernel(
    x_ref, obs_hbm, rw_hbm, model_hbm, smooth_hbm, active_hbm,
    out_ref,
    obs_ref, rw_ref, model_ref, smooth_ref, active_ref, raw, halves, md, mt, mbuf, dbuf, ubuf, halo, smbuf, sdbuf,
    free, weight, smooth_s, x_s, r_s, p_s, s_s, z_s, rs_s, rr_s, base, coef, fs_s, fr_s, scal,
    small_sem, load_sem, m_send, m_recv, d_send, d_recv, h_send, h_recv, s_send, s_recv,
):
    dp = lax.axis_index("dp")
    mp = lax.axis_index("mp")
    gravity = dp < DP * 3 // 4

    smalls = [
        pltpu.make_async_copy(src, dst, small_sem.at[k])
        for k, (src, dst) in enumerate(
            [
                (model_hbm, model_ref),
                (active_hbm, active_ref),
                (smooth_hbm, smooth_ref),
                (obs_hbm, obs_ref),
                (rw_hbm, rw_ref),
            ]
        )
    ]
    smalls[0].start()
    loads = [
        pltpu.make_async_copy(
            x_ref.at[pl.ds(k * CHUNK * 16, CHUNK * 16)],
            raw.at[pl.ds(k * CHUNK * 16, CHUNK * 16)],
            load_sem.at[k],
        )
        for k in range(CHUNKS)
    ]
    for load in loads:
        load.start()
    for small in smalls[1:]:
        small.start()

    m_peers = far_first(mp, MP // 4, 4, lambda other: {"dp": dp, "mp": other})
    d_peers = far_first(dp, 4, DP // 4, lambda other: {"dp": other, "mp": mp})
    barrier = pltpu.get_barrier_semaphore()
    for peer in m_peers + d_peers:
        pl.semaphore_signal(barrier, inc=1, device_id=peer, device_id_type=MESH)

    smalls[0].wait()
    for layer in range(2):
        for field in range(2):
            at = pl.ds(field * 16 + layer, 8, stride=2)
            ubuf[0, layer * 2 + field] = model_ref[at, :]
    for ref in (x_s, p_s, s_s, z_s, rs_s):
        ref[...] = jnp.zeros_like(ref)
    fs_s[...] = jnp.zeros_like(fs_s)
    sdbuf[dp] = jnp.zeros((8, 128), F32)

    def chosen(u):
        return [jnp.where(gravity, u[layer * 2], u[layer * 2 + 1]) for layer in range(2)]

    first = [tile.astype(BF16) for tile in chosen(ubuf[0])]
    for k in range(CHUNKS):
        loads[k].wait()
        block = raw[pl.ds(k * CHUNK * 16, CHUNK * 16), :].reshape(CHUNK, 16, 128)
        turned = jnp.swapaxes(block, 0, 1)
        acc = jnp.zeros((CHUNK, 128), F32)
        for c in range(8):
            terms = []
            for layer in range(2):
                at = (layer * 8 + c) * 128
                part = turned[c * 2 + layer]
                md[pl.ds(k * CHUNK, CHUNK), at : at + 128] = part
                terms.append(part * first[layer][c : c + 1])
            acc += (terms[0] + terms[1]).astype(F32)
        high = acc.astype(BF16)
        halves[pl.ds(k * CHUNK, CHUNK), :128] = high
        halves[pl.ds(k * CHUNK, CHUNK), 128:] = (acc - high.astype(F32)).astype(BF16)
    ones = jnp.ones((16, 256), BF16)
    sums = lax.dot_general(ones, halves[...], (((1,), (1,)), ((), ())), preferred_element_type=F32)
    for c in range(8):
        mbuf[0, mp, c : c + 1, :] = sums[0:1, c * 128 : c * 128 + 128]
    mbuf[0, mp, 8:9, :] = jnp.zeros((1, 128), F32)

    pl.semaphore_wait(barrier, MP - 1 + DP - 1)
    scalar_blocks = [smbuf.at[pl.ds(0, MP - 1), pl.ds(0, SROWS)], sdbuf.at[pl.ds(0, DP - 1)]]

    def step(k, carry):
        now = lax.rem(k, 2)
        later = 1 - now

        mine = mbuf.at[now, mp, pl.ds(0, MROWS)]
        for peer in m_peers:
            pltpu.make_async_remote_copy(
                src_ref=mine, dst_ref=mine, send_sem=m_send.at[now], recv_sem=m_recv.at[now],
                device_id=peer, device_id_type=MESH,
            ).start()
        halo_copies = []
        for side, (first, peer) in enumerate(
            [(2, {"dp": dp, "mp": lax.rem(mp + 1, MP)}), (0, {"dp": dp, "mp": lax.rem(mp + MP - 1, MP)})]
        ):
            copy = pltpu.make_async_remote_copy(
                src_ref=ubuf.at[now, pl.ds(first, 2)], dst_ref=halo.at[now, side],
                send_sem=h_send.at[side], recv_sem=h_recv.at[now, side],
                device_id=peer, device_id_type=MESH,
            )
            copy.start()
            halo_copies.append(copy)

        @pl.when(k == 0)
        def _():
            row = lax.broadcasted_iota(jnp.int32, (256, 256), 0)
            col = lax.broadcasted_iota(jnp.int32, (256, 256), 1)
            eye = jnp.where(row == col, 1.0, 0.0).astype(BF16)

            def turn(j, carry):
                at = pl.multiple_of(j * 256, 256)
                turned = lax.dot_general(
                    eye, md[:, pl.ds(at, 256)], (((1,), (1,)), ((), ())), preferred_element_type=F32
                )
                mt[pl.ds(at, 256), :] = turned.astype(BF16)
                return carry

            lax.fori_loop(0, CELLS // 256, turn, 0)
            for small in smalls[1:]:
                small.wait()
            for layer in range(2):
                weight[layer] = smooth_ref[pl.ds(layer, 8, stride=2), :]
                for field in range(2):
                    at = pl.ds(field * 16 + layer, 8, stride=2)
                    free[layer * 2 + field] = 1.0 - active_ref[at, :].astype(F32)

        u = ubuf[now]
        mask = free[...]

        def regularize():
            for copy in halo_copies:
                copy.wait()
            below = jnp.where(mp > 0, halo[now, 0], 0.0)
            above = jnp.where(mp < MP - 1, halo[now, 1], 0.0)
            smooth = regular(u, below, above, weight[...])
            smooth_s[...] = smooth
            return smooth

        @pl.when(k == STEPS - 1)
        def _():
            smooth = regularize()
            r, s, rr, rs = r_s[...], s_s[...], rr_s[...], rs_s[...]
            pairs_of = [(r, r), (u, r), (s, r), (u, u), (u, s), (s, s), (r, rr), (u, rr), (s, rr), (u, smooth), (u, rs), (s, rs)]
            for j, (one, two) in enumerate(pairs_of):
                smbuf[mp, j : j + 1] = lanes_of(one * two)
            mine_s = smbuf.at[mp, pl.ds(0, SROWS)]
            for peer in m_peers:
                pltpu.make_async_remote_copy(
                    src_ref=mine_s, dst_ref=mine_s, send_sem=s_send.at[0], recv_sem=s_recv.at[0],
                    device_id=peer, device_id_type=MESH,
                ).start()

        all_m = mbuf.at[now, pl.ds(0, MP - 1), pl.ds(0, MROWS)]
        pltpu.make_async_copy(all_m, all_m, m_recv.at[now]).wait()
        rows = mbuf[now, 0, 0:8]
        sums = mbuf[now, 0, 8:9]
        for j in range(1, MP):
            rows += mbuf[now, j, 0:8]
            sums += mbuf[now, j, 8:9]

        scaled = rw_ref[...] * (rows - jnp.where(k == 0, obs_ref[...], 0.0))
        columns = product([scaled], md, CELLS - 512)
        dbuf[now, dp, 0:8] = gathered(columns[:8])
        dbuf[now, dp, 8:16] = gathered(columns[8:])
        mine_d = dbuf.at[now, dp]
        for peer in d_peers:
            pltpu.make_async_remote_copy(
                src_ref=mine_d, dst_ref=mine_d, send_sem=d_send.at[now], recv_sem=d_recv.at[now],
                device_id=peer, device_id_type=MESH,
            ).start()

        @pl.when(k < STEPS - 1)
        def _():
            regularize()

        @pl.when(k == STEPS - 1)
        def _():
            fr, fs = fr_s[...], fs_s[...]
            for j, (one, two) in enumerate([(fr, fr), (rows, fr), (fs, fr), (rows, rows), (rows, fs), (fs, fs)]):
                sdbuf[dp, j : j + 1] = jnp.sum(rw_ref[...] * one * two, axis=0, keepdims=True)
            mine_e = sdbuf.at[dp]
            for peer in d_peers:
                pltpu.make_async_remote_copy(
                    src_ref=mine_e, dst_ref=mine_e, send_sem=s_send.at[1], recv_sem=s_recv.at[1],
                    device_id=peer, device_id_type=MESH,
                ).start()

        smooth = smooth_s[...]

        @pl.when(k == 0)
        def _():
            base[...] = -(mask * smooth)
            coef[...] = -mask

        @pl.when(k == 1)
        def _():
            r_s[...] = u
            fr_s[...] = rows
            rr_s[...] = smooth
            base[...] = mask * smooth
            coef[...] = mask

        @pl.when(k >= 2)
        def _():
            gamma, delta = split_sums(sums)
            first = k == 2
            beta = jnp.where(first, 0.0, gamma / jnp.where(first, 1.0, scal[0, 0:1, 0:1]))
            past = beta * gamma / jnp.where(first, 1.0, scal[1, 0:1, 0:1])
            alpha = gamma / (delta - past)
            scal[0] = jnp.broadcast_to(gamma, (8, 128))
            scal[1] = jnp.broadcast_to(alpha, (8, 128))
            scal[2] = jnp.broadcast_to(beta, (8, 128))
            r = r_s[...]
            p = r + beta * p_s[...]
            s = u + beta * s_s[...]
            r = r - alpha * s
            p_s[...] = p
            s_s[...] = s
            r_s[...] = r
            x_s[...] = x_s[...] + alpha * p
            fs = rows + beta * fs_s[...]
            fr = fr_s[...] - alpha * fs
            fs_s[...] = fs
            fr_s[...] = fr
            rs = smooth + beta * rs_s[...]
            rr = rr_s[...] - alpha * rs
            rs_s[...] = rs
            rr_s[...] = rr
            zb = mask * smooth + beta * z_s[...]
            z_s[...] = zb
            base[...] = u - alpha * zb
            coef[...] = -(alpha * mask)

        @pl.when(k == STEPS - 1)
        def _():
            for n, others in enumerate(scalar_blocks):
                pltpu.make_async_copy(others, others, s_recv.at[n]).wait()
            dots = smbuf[0, 0:SROWS]
            for j in range(1, MP):
                dots += smbuf[j, 0:SROWS]
            weighed = sdbuf[0]
            for j in range(1, DP):
                weighed += sdbuf[j]
            a, b, g = scal[1, 0:1, 0:1], scal[2, 0:1, 0:1], scal[0, 0:1, 0:1]

            def after(rows):
                rr, wr, sr, ww, ws, ss = (rows[j : j + 1] for j in range(6))
                terms = rr - (2.0 * a) * (wr + b * sr) + (a * a) * (ww + (2.0 * b) * ws + (b * b) * ss)
                return jnp.sum(terms, axis=1, keepdims=True)

            gamma = after(dots[0:6])
            delta = after(dots[6:12]) + after(weighed[0:6])
            beta = gamma / g
            alpha = gamma / (delta - beta * gamma / a)
            r = r_s[...]
            upd = x_s[...] + alpha * (r + beta * p_s[...])
            base[...] = r - alpha * (beta * s_s[...] + base[...])
            coef[...] = -(alpha * coef[...])
            for layer in range(2):
                for field in range(2):
                    out_ref[0, pl.ds(field * 16 + layer, 8, stride=2), :] = upd[layer * 2 + field]

        pltpu.make_async_copy(all_m, all_m, m_send.at[now]).wait()
        all_d = dbuf.at[now, pl.ds(0, DP - 1)]
        pltpu.make_async_copy(all_d, all_d, d_recv.at[now]).wait()
        density = dbuf[now, 0]
        for j in range(1, 6):
            density += dbuf[now, j]
        suscept = dbuf[now, 6] + dbuf[now, 7]
        summed = jnp.stack([density[:8], suscept[:8], density[8:], suscept[8:]])
        v = base[...] + coef[...] * summed
        ubuf[later] = v
        z_s[...] = z_s[...] + jnp.where(k >= 2, mask, 0.0) * summed

        @pl.when(k < STEPS - 1)
        def _():
            mbuf[later, mp, 0:8] = gathered(product(chosen(v), mt, ROWS - 256))
            r = r_s[...]
            mbuf[later, mp, 8:9] = two_sums(lanes_of(r * r), lanes_of(r * v))

        pltpu.make_async_copy(all_d, all_d, d_send.at[now]).wait()
        return carry

    r_s[...] = jnp.zeros_like(r_s)
    lax.fori_loop(0, STEPS, step, 0)

    res = ubuf[STEPS % 2]
    for layer in range(2):
        for field in range(2):
            out_ref[1, pl.ds(field * 16 + layer, 8, stride=2), :] = res[layer * 2 + field]
    for n, others in enumerate(scalar_blocks):
        pltpu.make_async_copy(others, others, s_send.at[n]).wait()


def pairs(field):
    lead = field.shape[:-2]
    n = len(lead)
    cut = field.reshape(*lead, 2, 8, 128)
    return jnp.swapaxes(cut, n, n + 1).reshape(-1, 128)


def unpairs(rows):
    return jnp.swapaxes(rows.reshape(2, 2, 8, 2, 128), 2, 3).reshape(2, 2, 2, 1024)


def local(sensitivity, observed, row_weight, model, smooth_weight, active):
    vmem = pl.BlockSpec(memory_space=pltpu.VMEM)
    cells = pltpu.VMEM((4, 8, 128), F32)
    tile = pltpu.VMEM((8, 128), F32)
    out = pl.pallas_call(
        kernel,
        out_shape=jax.ShapeDtypeStruct((2, 32, 128), F32),
        in_specs=[pl.BlockSpec(memory_space=pltpu.HBM)] * 6,
        out_specs=vmem,
        scratch_shapes=[
            tile, tile,
            pltpu.VMEM((32, 128), F32),
            pltpu.VMEM((16, 128), F32),
            pltpu.VMEM((32, 128), jnp.int32),
            pltpu.VMEM((ROWS * 16, 128), BF16),
            pltpu.VMEM((ROWS, 256), BF16),
            pltpu.VMEM((ROWS, CELLS), BF16),
            pltpu.VMEM((CELLS, ROWS), BF16),
            pltpu.VMEM((2, MP, 16, 128), F32),
            pltpu.VMEM((2, DP, 16, 128), F32),
            pltpu.VMEM((2, 4, 8, 128), F32),
            pltpu.VMEM((2, 2, 2, 8, 128), F32),
            pltpu.VMEM((MP, 16, 128), F32),
            pltpu.VMEM((DP, 8, 128), F32),
            cells,
            pltpu.VMEM((2, 8, 128), F32),
            cells, cells, cells, cells, cells, cells, cells, cells, cells, cells,
            tile, tile,
            pltpu.VMEM((3, 8, 128), F32),
            pltpu.SemaphoreType.DMA((5,)),
            pltpu.SemaphoreType.DMA((CHUNKS,)),
            pltpu.SemaphoreType.DMA((2,)),
            pltpu.SemaphoreType.DMA((2,)),
            pltpu.SemaphoreType.DMA((2,)),
            pltpu.SemaphoreType.DMA((2,)),
            pltpu.SemaphoreType.DMA((2,)),
            pltpu.SemaphoreType.DMA((2, 2)),
            pltpu.SemaphoreType.DMA((2,)),
            pltpu.SemaphoreType.DMA((2,)),
        ],
        compiler_params=pltpu.CompilerParams(
            collective_id=0, has_side_effects=True, vmem_limit_bytes=32 * 2**20
        ),
    )(
        *(
            pltpu.with_memory_space_constraint(x, pltpu.HBM)
            for x in (
                pairs(sensitivity),
                observed.reshape(8, 128),
                row_weight.reshape(8, 128),
                pairs(model),
                pairs(smooth_weight),
                pairs(active),
            )
        )
    )
    both = unpairs(out)
    return both[0], both[1]


def solution(mesh):
    return jax.shard_map(
        local,
        mesh=mesh,
        in_specs=(
            P("dp", "mp", None),
            P("dp"),
            P("dp"),
            P(None, "mp", None),
            P("mp", None),
            P(None, "mp", None),
        ),
        out_specs=(P(None, "mp", None), P(None, "mp", None)),
        check_vma=False,
    )
```

```python
import functools

import jax
import jax.numpy as jnp
from jax import lax
from jax.experimental import pallas as pl
from jax.experimental.pallas import tpu as pltpu
from jax.sharding import PartitionSpec as P

MESH = pl.DeviceIdType.MESH
F32 = jnp.float32
BF16 = jnp.bfloat16

GZ = 16
STEPS = 5
SMOOTHING = 0.25
COUPLING = 0.5

ROWS = 1024
CELLS = 2048
CHUNK = 128
CHUNKS = ROWS // CHUNK
DP = 8
MP = 16
MROWS = 9
SROWS = 12


def far_first(me, outer, inner, place):
    high, low = me // inner, lax.rem(me, inner)
    steps = [(a, b) for a in range(outer) for b in range(inner) if a or b]
    steps.sort(key=lambda s: -(min(s[0], outer - s[0]) + min(s[1], inner - s[1])))
    return [place(lax.rem(high + a, outer) * inner + lax.rem(low + b, inner)) for a, b in steps]


def spread(tiles):
    parts = []
    for tile in tiles:
        high = tile.astype(BF16).astype(F32)
        low = tile - high
        for c in range(8):
            both = jnp.concatenate(
                [
                    jnp.broadcast_to(high[c : c + 1], (8, 128)),
                    jnp.broadcast_to(low[c : c + 1], (8, 128)),
                ],
                axis=0,
            )
            parts.append(both.astype(BF16))
    return jnp.concatenate(parts, axis=1)


def product(tiles, matrix, split):
    width = matrix.shape[1]
    sums = [None] * ((width - split) // 128)
    for q in range(matrix.shape[0] // 128):
        row = tiles[q // 8][q % 8 : q % 8 + 1]
        column = jnp.transpose(jnp.broadcast_to(row, (128, 128)))
        for j in range(len(sums)):
            at = split + j * 128
            term = matrix[pl.ds(q * 128, 128), at : at + 128].astype(F32) * column
            term = jnp.sum(term.reshape(16, 8, 128), axis=0)
            sums[j] = term if sums[j] is None else sums[j] + term
    both = jnp.dot(spread(tiles), matrix[:, :split], preferred_element_type=F32)
    total = both[:8] + both[8:]
    outs = [total[:, at : at + 128] for at in range(0, split, 128)]
    return outs + [jnp.broadcast_to(jnp.sum(one, axis=0, keepdims=True), (8, 128)) for one in sums]


def gathered(outs):
    sub = lax.broadcasted_iota(jnp.int32, (8, 128), 0)
    tile = outs[0]
    for c in range(1, 8):
        tile = jnp.where(sub == c, outs[c], tile)
    return tile


def fold(one, two, gap):
    upper = lax.broadcasted_iota(jnp.int32, (8, 128), 0) // gap % 2 == 1
    kept = jnp.where(upper, two, one)
    moved = jnp.where(upper, one, two)
    if gap == 4:
        return kept + pltpu.roll(moved, 4, 0)
    return kept + jnp.where(upper, pltpu.roll(moved, gap, 0), pltpu.roll(moved, 8 - gap, 0))


def regular(u, below, above, weight):
    lane = lax.broadcasted_iota(jnp.int32, (8, 128), 1)
    sub = lax.broadcasted_iota(jnp.int32, (8, 128), 0)
    outs = []
    for layer in range(2):
        for field in range(2):
            v = u[layer * 2 + field]
            beside = u[(1 - layer) * 2 + field] + (below[field] if layer == 0 else above[field])
            beside += jnp.where(lane % GZ != GZ - 1, pltpu.roll(v, 127, 1), 0.0)
            beside += jnp.where(lane % GZ != 0, pltpu.roll(v, 1, 1), 0.0)
            later = pltpu.roll(v, 128 - GZ, 1)
            wrapped = jnp.where(sub < 7, pltpu.roll(later, 7, 0), 0.0)
            beside += jnp.where(lane < 128 - GZ, later, wrapped)
            earlier = pltpu.roll(v, GZ, 1)
            wrapped = jnp.where(sub > 0, pltpu.roll(earlier, 1, 0), 0.0)
            beside += jnp.where(lane >= GZ, earlier, wrapped)
            other = u[layer * 2 + 1 - field]
            outs.append(weight[layer] * v + SMOOTHING * (6.0 * v - beside) + COUPLING * (v - other))
    return jnp.stack(outs)


def lanes_of(cells):
    return jnp.sum(jnp.sum(cells, axis=0), axis=0, keepdims=True)


def two_sums(one, two):
    lane = lax.broadcasted_iota(jnp.int32, (1, 128), 1)
    return jnp.where(lane < 64, one + pltpu.roll(one, 64, 1), two + pltpu.roll(two, 64, 1))


def split_sums(row):
    lane = lax.broadcasted_iota(jnp.int32, (1, 128), 1)
    one = jnp.sum(jnp.where(lane < 64, row, 0.0), axis=1, keepdims=True)
    two = jnp.sum(jnp.where(lane < 64, 0.0, row), axis=1, keepdims=True)
    return one, two


def kernel(
    x_ref, obs_hbm, rw_hbm, model_hbm, smooth_hbm, active_hbm,
    out_ref,
    obs_ref, rw_ref, model_ref, smooth_ref, active_ref, raw, halves, md, mt, mbuf, dbuf, ubuf, halo, smbuf, sdbuf,
    free, weight, smooth_s, x_s, r_s, p_s, s_s, z_s, rs_s, rr_s, base, coef, fs_s, fr_s, scal,
    small_sem, load_sem, m_send, m_recv, d_send, d_recv, h_send, h_recv, s_send, s_recv,
):
    dp = lax.axis_index("dp")
    mp = lax.axis_index("mp")
    gravity = dp < DP * 3 // 4

    m_peers = far_first(mp, MP // 4, 4, lambda other: {"dp": dp, "mp": other})
    d_peers = far_first(dp, 4, DP // 4, lambda other: {"dp": other, "mp": mp})
    barrier = pltpu.get_barrier_semaphore()
    for peer in m_peers + d_peers:
        pl.semaphore_signal(barrier, inc=1, device_id=peer, device_id_type=MESH)

    smalls = [
        pltpu.make_async_copy(src, dst, small_sem.at[k])
        for k, (src, dst) in enumerate(
            [
                (model_hbm, model_ref),
                (active_hbm, active_ref),
                (smooth_hbm, smooth_ref),
                (obs_hbm, obs_ref),
                (rw_hbm, rw_ref),
            ]
        )
    ]
    smalls[0].start()
    def load(k):
        at = pl.ds(pl.multiple_of(k * (CHUNK * 16), CHUNK * 16), CHUNK * 16)
        return pltpu.make_async_copy(x_ref.at[at], raw.at[at], load_sem.at[k])

    for k in range(CHUNKS):
        load(k).start()
    for small in smalls[1:]:
        small.start()

    smalls[0].wait()
    for layer in range(2):
        for field in range(2):
            at = pl.ds(field * 16 + layer, 8, stride=2)
            ubuf[0, layer * 2 + field] = model_ref[at, :]
    for ref in (x_s, p_s, s_s, z_s, rs_s):
        ref[...] = jnp.zeros_like(ref)
    fs_s[...] = jnp.zeros_like(fs_s)
    sdbuf[dp] = jnp.zeros((8, 128), F32)

    def chosen(u):
        return [jnp.where(gravity, u[layer * 2], u[layer * 2 + 1]) for layer in range(2)]

    first = jnp.where(gravity, model_ref[0:16, :], model_ref[16:32, :]).astype(BF16)

    def multiply(k, carry):
        load(k).wait()
        for group in range(CHUNK // 16):
            folded = []
            for half in range(2):
                rows = []
                for r in range(8):
                    at = k * CHUNK + group * 16 + half * 8 + r
                    terms = (raw[pl.ds(pl.multiple_of(at * 16, 16), 16), :] * first).astype(F32)
                    rows.append(terms[:8] + terms[8:])
                for gap in (4, 2, 1):
                    rows = [fold(rows[j], rows[j + gap], gap) for j in range(gap)]
                folded.append(rows[0])
            acc = jnp.concatenate(folded, axis=0)
            here = pl.ds(pl.multiple_of(k * CHUNK + group * 16, 16), 16)
            high = acc.astype(BF16)
            halves[here, :128] = high
            halves[here, 128:] = (acc - high.astype(F32)).astype(BF16)
        return carry

    lax.fori_loop(0, CHUNKS, multiply, 0)
    ones = jnp.ones((16, 256), BF16)
    sums = lax.dot_general(ones, halves[...], (((1,), (1,)), ((), ())), preferred_element_type=F32)
    for c in range(8):
        mbuf[0, mp, c : c + 1, :] = sums[0:1, c * 128 : c * 128 + 128]
    mbuf[0, mp, 8:9, :] = jnp.zeros((1, 128), F32)

    pl.semaphore_wait(barrier, MP - 1 + DP - 1)
    scalar_blocks = [smbuf.at[pl.ds(0, MP - 1), pl.ds(0, SROWS)], sdbuf.at[pl.ds(0, DP - 1)]]

    def step(k, carry):
        now = lax.rem(k, 2)
        later = 1 - now

        mine = mbuf.at[now, mp, pl.ds(0, MROWS)]
        for peer in m_peers:
            pltpu.make_async_remote_copy(
                src_ref=mine, dst_ref=mine, send_sem=m_send.at[now], recv_sem=m_recv.at[now],
                device_id=peer, device_id_type=MESH,
            ).start()
        halo_copies = []
        for side, (first, peer) in enumerate(
            [(2, {"dp": dp, "mp": lax.rem(mp + 1, MP)}), (0, {"dp": dp, "mp": lax.rem(mp + MP - 1, MP)})]
        ):
            copy = pltpu.make_async_remote_copy(
                src_ref=ubuf.at[now, pl.ds(first, 2)], dst_ref=halo.at[now, side],
                send_sem=h_send.at[side], recv_sem=h_recv.at[now, side],
                device_id=peer, device_id_type=MESH,
            )
            copy.start()
            halo_copies.append(copy)

        def turn_some(low, high):
            row = lax.broadcasted_iota(jnp.int32, (256, 256), 0)
            col = lax.broadcasted_iota(jnp.int32, (256, 256), 1)
            eye = jnp.where(row == col, 1.0, 0.0).astype(BF16)

            def turn(j, carry):
                at = pl.multiple_of(j * 256, 256)
                turned = lax.dot_general(
                    eye, md[:, pl.ds(at, 256)], (((1,), (1,)), ((), ())), preferred_element_type=F32
                )
                mt[pl.ds(at, 256), :] = turned.astype(BF16)
                return carry

            lax.fori_loop(low, high, turn, 0)

        @pl.when(k == 0)
        def _():
            def arrange(j, carry):
                block = raw[pl.ds(pl.multiple_of(j * 2048, 2048), 2048), :].reshape(128, 16, 128)
                turned = jnp.swapaxes(block, 0, 1)
                for c in range(8):
                    for layer in range(2):
                        at = (layer * 8 + c) * 128
                        md[pl.ds(pl.multiple_of(j * 128, 128), 128), at : at + 128] = turned[c * 2 + layer]
                return carry

            lax.fori_loop(0, ROWS // 128, arrange, 0)
            turn_some(0, CELLS // 512)
            for small in smalls[1:]:
                small.wait()
            for layer in range(2):
                weight[layer] = smooth_ref[pl.ds(layer, 8, stride=2), :]
                for field in range(2):
                    at = pl.ds(field * 16 + layer, 8, stride=2)
                    free[layer * 2 + field] = 1.0 - active_ref[at, :].astype(F32)

        u = ubuf[now]
        mask = free[...]

        def regularize():
            for copy in halo_copies:
                copy.wait()
            below = jnp.where(mp > 0, halo[now, 0], 0.0)
            above = jnp.where(mp < MP - 1, halo[now, 1], 0.0)
            smooth = regular(u, below, above, weight[...])
            smooth_s[...] = smooth
            return smooth

        @pl.when(k == STEPS - 1)
        def _():
            smooth = regularize()
            r, s, rr, rs = r_s[...], s_s[...], rr_s[...], rs_s[...]
            pairs_of = [(r, r), (u, r), (s, r), (u, u), (u, s), (s, s), (r, rr), (u, rr), (s, rr), (u, smooth), (u, rs), (s, rs)]
            for j, (one, two) in enumerate(pairs_of):
                smbuf[mp, j : j + 1] = lanes_of(one * two)
            mine_s = smbuf.at[mp, pl.ds(0, SROWS)]
            for peer in m_peers:
                pltpu.make_async_remote_copy(
                    src_ref=mine_s, dst_ref=mine_s, send_sem=s_send.at[0], recv_sem=s_recv.at[0],
                    device_id=peer, device_id_type=MESH,
                ).start()

        all_m = mbuf.at[now, pl.ds(0, MP - 1), pl.ds(0, MROWS)]
        pltpu.make_async_copy(all_m, all_m, m_recv.at[now]).wait()
        rows = mbuf[now, 0, 0:8]
        sums = mbuf[now, 0, 8:9]
        for j in range(1, MP):
            rows += mbuf[now, j, 0:8]
            sums += mbuf[now, j, 8:9]

        scaled = rw_ref[...] * (rows - jnp.where(k == 0, obs_ref[...], 0.0))
        columns = product([scaled], md, CELLS - 512)
        dbuf[now, dp, 0:8] = gathered(columns[:8])
        dbuf[now, dp, 8:16] = gathered(columns[8:])
        mine_d = dbuf.at[now, dp]
        for peer in d_peers:
            pltpu.make_async_remote_copy(
                src_ref=mine_d, dst_ref=mine_d, send_sem=d_send.at[now], recv_sem=d_recv.at[now],
                device_id=peer, device_id_type=MESH,
            ).start()

        @pl.when(k < STEPS - 1)
        def _():
            regularize()

        @pl.when(k == 0)
        def _():
            turn_some(CELLS // 512, CELLS // 256)

        @pl.when(k == STEPS - 1)
        def _():
            fr, fs = fr_s[...], fs_s[...]
            for j, (one, two) in enumerate([(fr, fr), (rows, fr), (fs, fr), (rows, rows), (rows, fs), (fs, fs)]):
                sdbuf[dp, j : j + 1] = jnp.sum(rw_ref[...] * one * two, axis=0, keepdims=True)
            mine_e = sdbuf.at[dp]
            for peer in d_peers:
                pltpu.make_async_remote_copy(
                    src_ref=mine_e, dst_ref=mine_e, send_sem=s_send.at[1], recv_sem=s_recv.at[1],
                    device_id=peer, device_id_type=MESH,
                ).start()

        smooth = smooth_s[...]

        @pl.when(k == 0)
        def _():
            base[...] = -(mask * smooth)
            coef[...] = -mask

        @pl.when(k == 1)
        def _():
            r_s[...] = u
            fr_s[...] = rows
            rr_s[...] = smooth
            base[...] = mask * smooth
            coef[...] = mask

        @pl.when(k >= 2)
        def _():
            gamma, delta = split_sums(sums)
            first = k == 2
            beta = jnp.where(first, 0.0, gamma / jnp.where(first, 1.0, scal[0, 0:1, 0:1]))
            past = beta * gamma / jnp.where(first, 1.0, scal[1, 0:1, 0:1])
            alpha = gamma / (delta - past)
            scal[0] = jnp.broadcast_to(gamma, (8, 128))
            scal[1] = jnp.broadcast_to(alpha, (8, 128))
            scal[2] = jnp.broadcast_to(beta, (8, 128))
            r = r_s[...]
            p = r + beta * p_s[...]
            s = u + beta * s_s[...]
            r = r - alpha * s
            p_s[...] = p
            s_s[...] = s
            r_s[...] = r
            x_s[...] = x_s[...] + alpha * p
            fs = rows + beta * fs_s[...]
            fr = fr_s[...] - alpha * fs
            fs_s[...] = fs
            fr_s[...] = fr
            rs = smooth + beta * rs_s[...]
            rr = rr_s[...] - alpha * rs
            rs_s[...] = rs
            rr_s[...] = rr
            zb = mask * smooth + beta * z_s[...]
            z_s[...] = zb
            base[...] = u - alpha * zb
            coef[...] = -(alpha * mask)

        @pl.when(k == STEPS - 1)
        def _():
            for n, others in enumerate(scalar_blocks):
                pltpu.make_async_copy(others, others, s_recv.at[n]).wait()
            dots = smbuf[0, 0:SROWS]
            for j in range(1, MP):
                dots += smbuf[j, 0:SROWS]
            weighed = sdbuf[0]
            for j in range(1, DP):
                weighed += sdbuf[j]
            a, b, g = scal[1, 0:1, 0:1], scal[2, 0:1, 0:1], scal[0, 0:1, 0:1]

            def after(rows):
                rr, wr, sr, ww, ws, ss = (rows[j : j + 1] for j in range(6))
                terms = rr - (2.0 * a) * (wr + b * sr) + (a * a) * (ww + (2.0 * b) * ws + (b * b) * ss)
                return jnp.sum(terms, axis=1, keepdims=True)

            gamma = after(dots[0:6])
            delta = after(dots[6:12]) + after(weighed[0:6])
            beta = gamma / g
            alpha = gamma / (delta - beta * gamma / a)
            r = r_s[...]
            upd = x_s[...] + alpha * (r + beta * p_s[...])
            base[...] = r - alpha * (beta * s_s[...] + base[...])
            coef[...] = -(alpha * coef[...])
            for layer in range(2):
                for field in range(2):
                    out_ref[0, pl.ds(field * 16 + layer, 8, stride=2), :] = upd[layer * 2 + field]

        pltpu.make_async_copy(all_m, all_m, m_send.at[now]).wait()
        all_d = dbuf.at[now, pl.ds(0, DP - 1)]
        pltpu.make_async_copy(all_d, all_d, d_recv.at[now]).wait()
        density = dbuf[now, 0]
        for j in range(1, 6):
            density += dbuf[now, j]
        suscept = dbuf[now, 6] + dbuf[now, 7]
        summed = jnp.stack([density[:8], suscept[:8], density[8:], suscept[8:]])
        v = base[...] + coef[...] * summed
        ubuf[later] = v
        z_s[...] = z_s[...] + jnp.where(k >= 2, mask, 0.0) * summed

        @pl.when(k < STEPS - 1)
        def _():
            mbuf[later, mp, 0:8] = gathered(product(chosen(v), mt, ROWS - 256))
            r = r_s[...]
            mbuf[later, mp, 8:9] = two_sums(lanes_of(r * r), lanes_of(r * v))

        pltpu.make_async_copy(all_d, all_d, d_send.at[now]).wait()
        return carry

    r_s[...] = jnp.zeros_like(r_s)
    lax.fori_loop(0, STEPS, step, 0)

    res = ubuf[STEPS % 2]
    for layer in range(2):
        for field in range(2):
            out_ref[1, pl.ds(field * 16 + layer, 8, stride=2), :] = res[layer * 2 + field]
    for n, others in enumerate(scalar_blocks):
        pltpu.make_async_copy(others, others, s_send.at[n]).wait()


def pairs(field):
    lead = field.shape[:-2]
    n = len(lead)
    cut = field.reshape(*lead, 2, 8, 128)
    return jnp.swapaxes(cut, n, n + 1).reshape(-1, 128)


def unpairs(rows):
    return jnp.swapaxes(rows.reshape(2, 2, 8, 2, 128), 2, 3).reshape(2, 2, 2, 1024)


def local(sensitivity, observed, row_weight, model, smooth_weight, active):
    vmem = pl.BlockSpec(memory_space=pltpu.VMEM)
    cells = pltpu.VMEM((4, 8, 128), F32)
    tile = pltpu.VMEM((8, 128), F32)
    out = pl.pallas_call(
        kernel,
        out_shape=jax.ShapeDtypeStruct((2, 32, 128), F32),
        in_specs=[pl.BlockSpec(memory_space=pltpu.HBM)] * 6,
        out_specs=vmem,
        scratch_shapes=[
            tile, tile,
            pltpu.VMEM((32, 128), F32),
            pltpu.VMEM((16, 128), F32),
            pltpu.VMEM((32, 128), jnp.int32),
            pltpu.VMEM((ROWS * 16, 128), BF16),
            pltpu.VMEM((ROWS, 256), BF16),
            pltpu.VMEM((ROWS, CELLS), BF16),
            pltpu.VMEM((CELLS, ROWS), BF16),
            pltpu.VMEM((2, MP, 16, 128), F32),
            pltpu.VMEM((2, DP, 16, 128), F32),
            pltpu.VMEM((2, 4, 8, 128), F32),
            pltpu.VMEM((2, 2, 2, 8, 128), F32),
            pltpu.VMEM((MP, 16, 128), F32),
            pltpu.VMEM((DP, 8, 128), F32),
            cells,
            pltpu.VMEM((2, 8, 128), F32),
            cells, cells, cells, cells, cells, cells, cells, cells, cells, cells,
            tile, tile,
            pltpu.VMEM((3, 8, 128), F32),
            pltpu.SemaphoreType.DMA((5,)),
            pltpu.SemaphoreType.DMA((CHUNKS,)),
            pltpu.SemaphoreType.DMA((2,)),
            pltpu.SemaphoreType.DMA((2,)),
            pltpu.SemaphoreType.DMA((2,)),
            pltpu.SemaphoreType.DMA((2,)),
            pltpu.SemaphoreType.DMA((2,)),
            pltpu.SemaphoreType.DMA((2, 2)),
            pltpu.SemaphoreType.DMA((2,)),
            pltpu.SemaphoreType.DMA((2,)),
        ],
        compiler_params=pltpu.CompilerParams(
            collective_id=0, has_side_effects=True, vmem_limit_bytes=32 * 2**20
        ),
    )(
        *(
            pltpu.with_memory_space_constraint(x, pltpu.HBM)
            for x in (
                pairs(sensitivity),
                observed.reshape(8, 128),
                row_weight.reshape(8, 128),
                pairs(model),
                pairs(smooth_weight),
                pairs(active),
            )
        )
    )
    both = unpairs(out)
    return both[0], both[1]


def solution(mesh):
    return jax.shard_map(
        local,
        mesh=mesh,
        in_specs=(
            P("dp", "mp", None),
            P("dp"),
            P("dp"),
            P(None, "mp", None),
            P("mp", None),
            P(None, "mp", None),
        ),
        out_specs=(P(None, "mp", None), P(None, "mp", None)),
        check_vma=False,
    )
```

```python
import functools

import jax
import jax.numpy as jnp
from jax import lax
from jax.experimental import pallas as pl
from jax.experimental.pallas import tpu as pltpu
from jax.sharding import PartitionSpec as P

MESH = pl.DeviceIdType.MESH
F32 = jnp.float32
BF16 = jnp.bfloat16

GZ = 16
STEPS = 5
SMOOTHING = 0.25
COUPLING = 0.5

ROWS = 1024
CELLS = 2048
CHUNK = 128
CHUNKS = ROWS // CHUNK
DP = 8
MP = 16
MROWS = 9
SROWS = 12


def far_first(me, outer, inner, place):
    high, low = me // inner, lax.rem(me, inner)
    steps = [(a, b) for a in range(outer) for b in range(inner) if a or b]
    steps.sort(key=lambda s: (-(min(s[0], outer - s[0]) + min(s[1], inner - s[1])), s[0] + s[1] > 4, s[1]))
    return [place(lax.rem(high + a, outer) * inner + lax.rem(low + b, inner)) for a, b in steps]


def spread(tiles):
    parts = []
    for tile in tiles:
        high = tile.astype(BF16).astype(F32)
        low = tile - high
        for c in range(8):
            both = jnp.concatenate(
                [
                    jnp.broadcast_to(high[c : c + 1], (8, 128)),
                    jnp.broadcast_to(low[c : c + 1], (8, 128)),
                ],
                axis=0,
            )
            parts.append(both.astype(BF16))
    return jnp.concatenate(parts, axis=1)


def product(tiles, matrix, split):
    width = matrix.shape[1]
    sums = [None] * ((width - split) // 128)
    for q in range(matrix.shape[0] // 128):
        row = tiles[q // 8][q % 8 : q % 8 + 1]
        column = jnp.transpose(jnp.broadcast_to(row, (128, 128)))
        for j in range(len(sums)):
            at = split + j * 128
            term = matrix[pl.ds(q * 128, 128), at : at + 128].astype(F32) * column
            term = jnp.sum(term.reshape(16, 8, 128), axis=0)
            sums[j] = term if sums[j] is None else sums[j] + term
    both = jnp.dot(spread(tiles), matrix[:, :split], preferred_element_type=F32)
    total = both[:8] + both[8:]
    outs = [total[:, at : at + 128] for at in range(0, split, 128)]
    return outs + [jnp.broadcast_to(jnp.sum(one, axis=0, keepdims=True), (8, 128)) for one in sums]


def gathered(outs):
    sub = lax.broadcasted_iota(jnp.int32, (8, 128), 0)
    tile = outs[0]
    for c in range(1, 8):
        tile = jnp.where(sub == c, outs[c], tile)
    return tile


def fold(one, two, gap):
    upper = lax.broadcasted_iota(jnp.int32, (8, 128), 0) // gap % 2 == 1
    kept = jnp.where(upper, two, one)
    moved = jnp.where(upper, one, two)
    if gap == 4:
        return kept + pltpu.roll(moved, 4, 0)
    return kept + jnp.where(upper, pltpu.roll(moved, gap, 0), pltpu.roll(moved, 8 - gap, 0))


def regular(u, below, above, weight):
    lane = lax.broadcasted_iota(jnp.int32, (8, 128), 1)
    sub = lax.broadcasted_iota(jnp.int32, (8, 128), 0)
    outs = []
    for layer in range(2):
        for field in range(2):
            v = u[layer * 2 + field]
            beside = u[(1 - layer) * 2 + field] + (below[field] if layer == 0 else above[field])
            beside += jnp.where(lane % GZ != GZ - 1, pltpu.roll(v, 127, 1), 0.0)
            beside += jnp.where(lane % GZ != 0, pltpu.roll(v, 1, 1), 0.0)
            later = pltpu.roll(v, 128 - GZ, 1)
            wrapped = jnp.where(sub < 7, pltpu.roll(later, 7, 0), 0.0)
            beside += jnp.where(lane < 128 - GZ, later, wrapped)
            earlier = pltpu.roll(v, GZ, 1)
            wrapped = jnp.where(sub > 0, pltpu.roll(earlier, 1, 0), 0.0)
            beside += jnp.where(lane >= GZ, earlier, wrapped)
            other = u[layer * 2 + 1 - field]
            outs.append(weight[layer] * v + SMOOTHING * (6.0 * v - beside) + COUPLING * (v - other))
    return jnp.stack(outs)


def lanes_of(cells):
    return jnp.sum(jnp.sum(cells, axis=0), axis=0, keepdims=True)


def two_sums(one, two):
    lane = lax.broadcasted_iota(jnp.int32, (1, 128), 1)
    return jnp.where(lane < 64, one + pltpu.roll(one, 64, 1), two + pltpu.roll(two, 64, 1))


def split_sums(row):
    lane = lax.broadcasted_iota(jnp.int32, (1, 128), 1)
    one = jnp.sum(jnp.where(lane < 64, row, 0.0), axis=1, keepdims=True)
    two = jnp.sum(jnp.where(lane < 64, 0.0, row), axis=1, keepdims=True)
    return one, two


def kernel(
    x_ref, obs_hbm, rw_hbm, model_hbm, smooth_hbm, active_hbm,
    out_ref,
    obs_ref, rw_ref, model_ref, smooth_ref, active_ref, raw, halves, md, mt, mbuf, dbuf, ubuf, halo, smbuf, sdbuf,
    free, weight, smooth_s, x_s, r_s, p_s, s_s, z_s, rs_s, rr_s, base, coef, fs_s, fr_s, scal,
    small_sem, load_sem, m_send, m_recv, d_send, d_recv, h_send, h_recv, s_send, s_recv,
):
    dp = lax.axis_index("dp")
    mp = lax.axis_index("mp")
    gravity = dp < DP * 3 // 4

    m_peers = far_first(mp, MP // 4, 4, lambda other: {"dp": dp, "mp": other})
    d_peers = far_first(dp, 4, DP // 4, lambda other: {"dp": other, "mp": mp})
    barrier = pltpu.get_barrier_semaphore()
    for peer in m_peers + d_peers:
        pl.semaphore_signal(barrier, inc=1, device_id=peer, device_id_type=MESH)

    smalls = [
        pltpu.make_async_copy(src, dst, small_sem.at[k])
        for k, (src, dst) in enumerate(
            [
                (model_hbm, model_ref),
                (active_hbm, active_ref),
                (smooth_hbm, smooth_ref),
                (obs_hbm, obs_ref),
                (rw_hbm, rw_ref),
            ]
        )
    ]
    smalls[0].start()
    def load(k):
        at = pl.ds(pl.multiple_of(k * (CHUNK * 16), CHUNK * 16), CHUNK * 16)
        return pltpu.make_async_copy(x_ref.at[at], raw.at[at], load_sem.at[k])

    for k in range(CHUNKS):
        load(k).start()
    for small in smalls[1:]:
        small.start()

    smalls[0].wait()
    for layer in range(2):
        for field in range(2):
            at = pl.ds(field * 16 + layer, 8, stride=2)
            ubuf[0, layer * 2 + field] = model_ref[at, :]
    for ref in (x_s, p_s, s_s, z_s, rs_s):
        ref[...] = jnp.zeros_like(ref)
    fs_s[...] = jnp.zeros_like(fs_s)
    sdbuf[dp] = jnp.zeros((8, 128), F32)

    def chosen(u):
        return [jnp.where(gravity, u[layer * 2], u[layer * 2 + 1]) for layer in range(2)]

    first = jnp.where(gravity, model_ref[0:16, :], model_ref[16:32, :]).astype(BF16)

    def multiply(k, carry):
        load(k).wait()
        for group in range(CHUNK // 16):
            folded = []
            for half in range(2):
                rows = []
                for r in range(8):
                    at = k * CHUNK + group * 16 + half * 8 + r
                    terms = (raw[pl.ds(pl.multiple_of(at * 16, 16), 16), :] * first).astype(F32)
                    rows.append(terms[:8] + terms[8:])
                for gap in (4, 2, 1):
                    rows = [fold(rows[j], rows[j + gap], gap) for j in range(gap)]
                folded.append(rows[0])
            acc = jnp.concatenate(folded, axis=0)
            here = pl.ds(pl.multiple_of(k * CHUNK + group * 16, 16), 16)
            high = acc.astype(BF16)
            halves[here, :128] = high
            halves[here, 128:] = (acc - high.astype(F32)).astype(BF16)
        return carry

    lax.fori_loop(0, CHUNKS, multiply, 0)
    ones = jnp.ones((16, 256), BF16)
    sums = lax.dot_general(ones, halves[...], (((1,), (1,)), ((), ())), preferred_element_type=F32)
    for c in range(8):
        mbuf[0, mp, c : c + 1, :] = sums[0:1, c * 128 : c * 128 + 128]
    mbuf[0, mp, 8:9, :] = jnp.zeros((1, 128), F32)

    pl.semaphore_wait(barrier, MP - 1 + DP - 1)
    scalar_blocks = [smbuf.at[pl.ds(0, MP - 1), pl.ds(0, SROWS)], sdbuf.at[pl.ds(0, DP - 1)]]

    def step(k, carry):
        now = lax.rem(k, 2)
        later = 1 - now

        mine = mbuf.at[now, mp, pl.ds(0, MROWS)]
        for peer in m_peers:
            pltpu.make_async_remote_copy(
                src_ref=mine, dst_ref=mine, send_sem=m_send.at[now], recv_sem=m_recv.at[now],
                device_id=peer, device_id_type=MESH,
            ).start()
        halo_copies = []
        for side, (first, peer) in enumerate(
            [(2, {"dp": dp, "mp": lax.rem(mp + 1, MP)}), (0, {"dp": dp, "mp": lax.rem(mp + MP - 1, MP)})]
        ):
            copy = pltpu.make_async_remote_copy(
                src_ref=ubuf.at[now, pl.ds(first, 2)], dst_ref=halo.at[now, side],
                send_sem=h_send.at[side], recv_sem=h_recv.at[now, side],
                device_id=peer, device_id_type=MESH,
            )
            copy.start()
            halo_copies.append(copy)

        def turn_some(low, high):
            row = lax.broadcasted_iota(jnp.int32, (256, 256), 0)
            col = lax.broadcasted_iota(jnp.int32, (256, 256), 1)
            eye = jnp.where(row == col, 1.0, 0.0).astype(BF16)

            def turn(j, carry):
                at = pl.multiple_of(j * 256, 256)
                turned = lax.dot_general(
                    eye, md[:, pl.ds(at, 256)], (((1,), (1,)), ((), ())), preferred_element_type=F32
                )
                mt[pl.ds(at, 256), :] = turned.astype(BF16)
                return carry

            lax.fori_loop(low, high, turn, 0)

        @pl.when(k == 0)
        def _():
            def arrange(j, carry):
                block = raw[pl.ds(pl.multiple_of(j * 2048, 2048), 2048), :].reshape(128, 16, 128)
                turned = jnp.swapaxes(block, 0, 1)
                for c in range(8):
                    for layer in range(2):
                        at = (layer * 8 + c) * 128
                        md[pl.ds(pl.multiple_of(j * 128, 128), 128), at : at + 128] = turned[c * 2 + layer]
                return carry

            lax.fori_loop(0, ROWS // 128, arrange, 0)
            turn_some(0, CELLS // 512)
            for small in smalls[1:]:
                small.wait()
            for layer in range(2):
                weight[layer] = smooth_ref[pl.ds(layer, 8, stride=2), :]
                for field in range(2):
                    at = pl.ds(field * 16 + layer, 8, stride=2)
                    free[layer * 2 + field] = 1.0 - active_ref[at, :].astype(F32)

        u = ubuf[now]
        mask = free[...]

        def regularize():
            for copy in halo_copies:
                copy.wait()
            below = jnp.where(mp > 0, halo[now, 0], 0.0)
            above = jnp.where(mp < MP - 1, halo[now, 1], 0.0)
            smooth = regular(u, below, above, weight[...])
            smooth_s[...] = smooth
            return smooth

        @pl.when(k == STEPS - 1)
        def _():
            smooth = regularize()
            r, s, rr, rs = r_s[...], s_s[...], rr_s[...], rs_s[...]
            pairs_of = [(r, r), (u, r), (s, r), (u, u), (u, s), (s, s), (r, rr), (u, rr), (s, rr), (u, smooth), (u, rs), (s, rs)]
            for j, (one, two) in enumerate(pairs_of):
                smbuf[mp, j : j + 1] = lanes_of(one * two)
            mine_s = smbuf.at[mp, pl.ds(0, SROWS)]
            for peer in m_peers:
                pltpu.make_async_remote_copy(
                    src_ref=mine_s, dst_ref=mine_s, send_sem=s_send.at[0], recv_sem=s_recv.at[0],
                    device_id=peer, device_id_type=MESH,
                ).start()

        all_m = mbuf.at[now, pl.ds(0, MP - 1), pl.ds(0, MROWS)]
        pltpu.make_async_copy(all_m, all_m, m_recv.at[now]).wait()
        rows = mbuf[now, 0, 0:8]
        sums = mbuf[now, 0, 8:9]
        for j in range(1, MP):
            rows += mbuf[now, j, 0:8]
            sums += mbuf[now, j, 8:9]

        scaled = rw_ref[...] * (rows - jnp.where(k == 0, obs_ref[...], 0.0))
        columns = product([scaled], md, CELLS - 512)
        dbuf[now, dp, 0:8] = gathered(columns[:8])
        dbuf[now, dp, 8:16] = gathered(columns[8:])
        mine_d = dbuf.at[now, dp]
        for peer in d_peers:
            pltpu.make_async_remote_copy(
                src_ref=mine_d, dst_ref=mine_d, send_sem=d_send.at[now], recv_sem=d_recv.at[now],
                device_id=peer, device_id_type=MESH,
            ).start()

        @pl.when(k < STEPS - 1)
        def _():
            regularize()

        @pl.when(k == 0)
        def _():
            turn_some(CELLS // 512, CELLS // 256)

        @pl.when(k == STEPS - 1)
        def _():
            fr, fs = fr_s[...], fs_s[...]
            for j, (one, two) in enumerate([(fr, fr), (rows, fr), (fs, fr), (rows, rows), (rows, fs), (fs, fs)]):
                sdbuf[dp, j : j + 1] = jnp.sum(rw_ref[...] * one * two, axis=0, keepdims=True)
            mine_e = sdbuf.at[dp]
            for peer in d_peers:
                pltpu.make_async_remote_copy(
                    src_ref=mine_e, dst_ref=mine_e, send_sem=s_send.at[1], recv_sem=s_recv.at[1],
                    device_id=peer, device_id_type=MESH,
                ).start()

        smooth = smooth_s[...]

        @pl.when(k == 0)
        def _():
            base[...] = -(mask * smooth)
            coef[...] = -mask

        @pl.when(k == 1)
        def _():
            r_s[...] = u
            fr_s[...] = rows
            rr_s[...] = smooth
            base[...] = mask * smooth
            coef[...] = mask

        @pl.when(k >= 2)
        def _():
            gamma, delta = split_sums(sums)
            first = k == 2
            beta = jnp.where(first, 0.0, gamma / jnp.where(first, 1.0, scal[0, 0:1, 0:1]))
            past = beta * gamma / jnp.where(first, 1.0, scal[1, 0:1, 0:1])
            alpha = gamma / (delta - past)
            scal[0] = jnp.broadcast_to(gamma, (8, 128))
            scal[1] = jnp.broadcast_to(alpha, (8, 128))
            scal[2] = jnp.broadcast_to(beta, (8, 128))
            r = r_s[...]
            p = r + beta * p_s[...]
            s = u + beta * s_s[...]
            r = r - alpha * s
            p_s[...] = p
            s_s[...] = s
            r_s[...] = r
            x_s[...] = x_s[...] + alpha * p
            fs = rows + beta * fs_s[...]
            fr = fr_s[...] - alpha * fs
            fs_s[...] = fs
            fr_s[...] = fr
            rs = smooth + beta * rs_s[...]
            rr = rr_s[...] - alpha * rs
            rs_s[...] = rs
            rr_s[...] = rr
            zb = mask * smooth + beta * z_s[...]
            z_s[...] = zb
            base[...] = u - alpha * zb
            coef[...] = -(alpha * mask)

        @pl.when(k == STEPS - 1)
        def _():
            for n, others in enumerate(scalar_blocks):
                pltpu.make_async_copy(others, others, s_recv.at[n]).wait()
            dots = smbuf[0, 0:SROWS]
            for j in range(1, MP):
                dots += smbuf[j, 0:SROWS]
            weighed = sdbuf[0]
            for j in range(1, DP):
                weighed += sdbuf[j]
            a, b, g = scal[1, 0:1, 0:1], scal[2, 0:1, 0:1], scal[0, 0:1, 0:1]

            def after(rows):
                rr, wr, sr, ww, ws, ss = (rows[j : j + 1] for j in range(6))
                terms = rr - (2.0 * a) * (wr + b * sr) + (a * a) * (ww + (2.0 * b) * ws + (b * b) * ss)
                return jnp.sum(terms, axis=1, keepdims=True)

            gamma = after(dots[0:6])
            delta = after(dots[6:12]) + after(weighed[0:6])
            beta = gamma / g
            alpha = gamma / (delta - beta * gamma / a)
            r = r_s[...]
            upd = x_s[...] + alpha * (r + beta * p_s[...])
            base[...] = r - alpha * (beta * s_s[...] + base[...])
            coef[...] = -(alpha * coef[...])
            for layer in range(2):
                for field in range(2):
                    out_ref[0, pl.ds(field * 16 + layer, 8, stride=2), :] = upd[layer * 2 + field]

        pltpu.make_async_copy(all_m, all_m, m_send.at[now]).wait()
        all_d = dbuf.at[now, pl.ds(0, DP - 1)]
        pltpu.make_async_copy(all_d, all_d, d_recv.at[now]).wait()
        density = dbuf[now, 0]
        for j in range(1, 6):
            density += dbuf[now, j]
        suscept = dbuf[now, 6] + dbuf[now, 7]
        summed = jnp.stack([density[:8], suscept[:8], density[8:], suscept[8:]])
        v = base[...] + coef[...] * summed
        ubuf[later] = v
        z_s[...] = z_s[...] + jnp.where(k >= 2, mask, 0.0) * summed

        @pl.when(k < STEPS - 1)
        def _():
            mbuf[later, mp, 0:8] = gathered(product(chosen(v), mt, ROWS - 256))
            r = r_s[...]
            mbuf[later, mp, 8:9] = two_sums(lanes_of(r * r), lanes_of(r * v))

        pltpu.make_async_copy(all_d, all_d, d_send.at[now]).wait()
        return carry

    r_s[...] = jnp.zeros_like(r_s)
    lax.fori_loop(0, STEPS, step, 0)

    res = ubuf[STEPS % 2]
    for layer in range(2):
        for field in range(2):
            out_ref[1, pl.ds(field * 16 + layer, 8, stride=2), :] = res[layer * 2 + field]
    for n, others in enumerate(scalar_blocks):
        pltpu.make_async_copy(others, others, s_send.at[n]).wait()


def pairs(field):
    lead = field.shape[:-2]
    n = len(lead)
    cut = field.reshape(*lead, 2, 8, 128)
    return jnp.swapaxes(cut, n, n + 1).reshape(-1, 128)


def unpairs(rows):
    return jnp.swapaxes(rows.reshape(2, 2, 8, 2, 128), 2, 3).reshape(2, 2, 2, 1024)


def local(sensitivity, observed, row_weight, model, smooth_weight, active):
    vmem = pl.BlockSpec(memory_space=pltpu.VMEM)
    cells = pltpu.VMEM((4, 8, 128), F32)
    tile = pltpu.VMEM((8, 128), F32)
    out = pl.pallas_call(
        kernel,
        out_shape=jax.ShapeDtypeStruct((2, 32, 128), F32),
        in_specs=[pl.BlockSpec(memory_space=pltpu.HBM)] * 6,
        out_specs=vmem,
        scratch_shapes=[
            tile, tile,
            pltpu.VMEM((32, 128), F32),
            pltpu.VMEM((16, 128), F32),
            pltpu.VMEM((32, 128), jnp.int32),
            pltpu.VMEM((ROWS * 16, 128), BF16),
            pltpu.VMEM((ROWS, 256), BF16),
            pltpu.VMEM((ROWS, CELLS), BF16),
            pltpu.VMEM((CELLS, ROWS), BF16),
            pltpu.VMEM((2, MP, 16, 128), F32),
            pltpu.VMEM((2, DP, 16, 128), F32),
            pltpu.VMEM((2, 4, 8, 128), F32),
            pltpu.VMEM((2, 2, 2, 8, 128), F32),
            pltpu.VMEM((MP, 16, 128), F32),
            pltpu.VMEM((DP, 8, 128), F32),
            cells,
            pltpu.VMEM((2, 8, 128), F32),
            cells, cells, cells, cells, cells, cells, cells, cells, cells, cells,
            tile, tile,
            pltpu.VMEM((3, 8, 128), F32),
            pltpu.SemaphoreType.DMA((5,)),
            pltpu.SemaphoreType.DMA((CHUNKS,)),
            pltpu.SemaphoreType.DMA((2,)),
            pltpu.SemaphoreType.DMA((2,)),
            pltpu.SemaphoreType.DMA((2,)),
            pltpu.SemaphoreType.DMA((2,)),
            pltpu.SemaphoreType.DMA((2,)),
            pltpu.SemaphoreType.DMA((2, 2)),
            pltpu.SemaphoreType.DMA((2,)),
            pltpu.SemaphoreType.DMA((2,)),
        ],
        compiler_params=pltpu.CompilerParams(
            collective_id=0, has_side_effects=True, vmem_limit_bytes=32 * 2**20
        ),
    )(
        *(
            pltpu.with_memory_space_constraint(x, pltpu.HBM)
            for x in (
                pairs(sensitivity),
                observed.reshape(8, 128),
                row_weight.reshape(8, 128),
                pairs(model),
                pairs(smooth_weight),
                pairs(active),
            )
        )
    )
    both = unpairs(out)
    return both[0], both[1]


def solution(mesh):
    return jax.shard_map(
        local,
        mesh=mesh,
        in_specs=(
            P("dp", "mp", None),
            P("dp"),
            P("dp"),
            P(None, "mp", None),
            P("mp", None),
            P(None, "mp", None),
        ),
        out_specs=(P(None, "mp", None), P(None, "mp", None)),
        check_vma=False,
    )
```

```python
import functools

import jax
import jax.numpy as jnp
from jax import lax
from jax.experimental import pallas as pl
from jax.experimental.pallas import tpu as pltpu
from jax.sharding import PartitionSpec as P

MESH = pl.DeviceIdType.MESH
F32 = jnp.float32
BF16 = jnp.bfloat16

GZ = 16
STEPS = 5
SMOOTHING = 0.25
COUPLING = 0.5

ROWS = 1024
CELLS = 2048
CHUNK = 256
CHUNKS = ROWS // CHUNK
DP = 8
MP = 16
MROWS = 9
SROWS = 12


def far_first(me, outer, inner, place):
    high, low = me // inner, lax.rem(me, inner)
    steps = [(a, b) for a in range(outer) for b in range(inner) if a or b]
    steps.sort(key=lambda s: -(min(s[0], outer - s[0]) + min(s[1], inner - s[1])))
    return [place(lax.rem(high + a, outer) * inner + lax.rem(low + b, inner)) for a, b in steps]


def spread(tiles):
    parts = []
    for tile in tiles:
        high = tile.astype(BF16).astype(F32)
        low = tile - high
        for c in range(8):
            both = jnp.concatenate(
                [
                    jnp.broadcast_to(high[c : c + 1], (8, 128)),
                    jnp.broadcast_to(low[c : c + 1], (8, 128)),
                ],
                axis=0,
            )
            parts.append(both.astype(BF16))
    return jnp.concatenate(parts, axis=1)


def product(tiles, matrix, split):
    width = matrix.shape[1]
    sums = [None] * ((width - split) // 128)
    for q in range(matrix.shape[0] // 128):
        row = tiles[q // 8][q % 8 : q % 8 + 1]
        column = jnp.transpose(jnp.broadcast_to(row, (128, 128)))
        for j in range(len(sums)):
            at = split + j * 128
            term = matrix[pl.ds(q * 128, 128), at : at + 128].astype(F32) * column
            term = jnp.sum(term.reshape(16, 8, 128), axis=0)
            sums[j] = term if sums[j] is None else sums[j] + term
    both = jnp.dot(spread(tiles), matrix[:, :split], preferred_element_type=F32)
    total = both[:8] + both[8:]
    outs = [total[:, at : at + 128] for at in range(0, split, 128)]
    return outs + [jnp.broadcast_to(jnp.sum(one, axis=0, keepdims=True), (8, 128)) for one in sums]


def gathered(outs):
    sub = lax.broadcasted_iota(jnp.int32, (8, 128), 0)
    tile = outs[0]
    for c in range(1, 8):
        tile = jnp.where(sub == c, outs[c], tile)
    return tile


def fold(one, two, gap):
    upper = lax.broadcasted_iota(jnp.int32, (8, 128), 0) // gap % 2 == 1
    kept = jnp.where(upper, two, one)
    moved = jnp.where(upper, one, two)
    if gap == 4:
        return kept + pltpu.roll(moved, 4, 0)
    return kept + jnp.where(upper, pltpu.roll(moved, gap, 0), pltpu.roll(moved, 8 - gap, 0))


def regular(u, below, above, weight):
    lane = lax.broadcasted_iota(jnp.int32, (8, 128), 1)
    sub = lax.broadcasted_iota(jnp.int32, (8, 128), 0)
    outs = []
    for layer in range(2):
        for field in range(2):
            v = u[layer * 2 + field]
            beside = u[(1 - layer) * 2 + field] + (below[field] if layer == 0 else above[field])
            beside += jnp.where(lane % GZ != GZ - 1, pltpu.roll(v, 127, 1), 0.0)
            beside += jnp.where(lane % GZ != 0, pltpu.roll(v, 1, 1), 0.0)
            later = pltpu.roll(v, 128 - GZ, 1)
            wrapped = jnp.where(sub < 7, pltpu.roll(later, 7, 0), 0.0)
            beside += jnp.where(lane < 128 - GZ, later, wrapped)
            earlier = pltpu.roll(v, GZ, 1)
            wrapped = jnp.where(sub > 0, pltpu.roll(earlier, 1, 0), 0.0)
            beside += jnp.where(lane >= GZ, earlier, wrapped)
            other = u[layer * 2 + 1 - field]
            outs.append(weight[layer] * v + SMOOTHING * (6.0 * v - beside) + COUPLING * (v - other))
    return jnp.stack(outs)


def lanes_of(cells):
    return jnp.sum(jnp.sum(cells, axis=0), axis=0, keepdims=True)


def two_sums(one, two):
    lane = lax.broadcasted_iota(jnp.int32, (1, 128), 1)
    return jnp.where(lane < 64, one + pltpu.roll(one, 64, 1), two + pltpu.roll(two, 64, 1))


def split_sums(row):
    lane = lax.broadcasted_iota(jnp.int32, (1, 128), 1)
    one = jnp.sum(jnp.where(lane < 64, row, 0.0), axis=1, keepdims=True)
    two = jnp.sum(jnp.where(lane < 64, 0.0, row), axis=1, keepdims=True)
    return one, two


def kernel(
    x_ref, obs_hbm, rw_hbm, model_hbm, smooth_hbm, active_hbm,
    out_ref,
    obs_ref, rw_ref, model_ref, smooth_ref, active_ref, raw, halves, md, mt, mbuf, dbuf, ubuf, halo, smbuf, sdbuf,
    free, weight, smooth_s, x_s, r_s, p_s, s_s, z_s, rs_s, rr_s, base, coef, fs_s, fr_s, scal,
    small_sem, load_sem, m_send, m_recv, d_send, d_recv, h_send, h_recv, s_send, s_recv,
):
    dp = lax.axis_index("dp")
    mp = lax.axis_index("mp")
    gravity = dp < DP * 3 // 4

    m_peers = far_first(mp, MP // 4, 4, lambda other: {"dp": dp, "mp": other})
    d_peers = far_first(dp, 4, DP // 4, lambda other: {"dp": other, "mp": mp})
    barrier = pltpu.get_barrier_semaphore()
    for peer in m_peers + d_peers:
        pl.semaphore_signal(barrier, inc=1, device_id=peer, device_id_type=MESH)

    smalls = [
        pltpu.make_async_copy(src, dst, small_sem.at[k])
        for k, (src, dst) in enumerate(
            [
                (model_hbm, model_ref),
                (active_hbm, active_ref),
                (smooth_hbm, smooth_ref),
                (obs_hbm, obs_ref),
                (rw_hbm, rw_ref),
            ]
        )
    ]
    smalls[0].start()
    def load(k):
        at = pl.ds(pl.multiple_of(k * (CHUNK * 16), CHUNK * 16), CHUNK * 16)
        return pltpu.make_async_copy(x_ref.at[at], raw.at[at], load_sem.at[k])

    for k in range(CHUNKS):
        load(k).start()
    for small in smalls[1:]:
        small.start()

    smalls[0].wait()
    for layer in range(2):
        for field in range(2):
            at = pl.ds(field * 16 + layer, 8, stride=2)
            ubuf[0, layer * 2 + field] = model_ref[at, :]
    for ref in (x_s, p_s, s_s, z_s, rs_s):
        ref[...] = jnp.zeros_like(ref)
    fs_s[...] = jnp.zeros_like(fs_s)
    sdbuf[dp] = jnp.zeros((8, 128), F32)

    def chosen(u):
        return [jnp.where(gravity, u[layer * 2], u[layer * 2 + 1]) for layer in range(2)]

    first = jnp.where(gravity, model_ref[0:16, :], model_ref[16:32, :]).astype(BF16)

    def multiply(k, carry):
        load(k).wait()
        for group in range(CHUNK // 16):
            folded = []
            for half in range(2):
                rows = []
                for r in range(8):
                    at = k * CHUNK + group * 16 + half * 8 + r
                    terms = (raw[pl.ds(pl.multiple_of(at * 16, 16), 16), :] * first).astype(F32)
                    rows.append(terms[:8] + terms[8:])
                for gap in (4, 2, 1):
                    rows = [fold(rows[j], rows[j + gap], gap) for j in range(gap)]
                folded.append(rows[0])
            acc = jnp.concatenate(folded, axis=0)
            here = pl.ds(pl.multiple_of(k * CHUNK + group * 16, 16), 16)
            high = acc.astype(BF16)
            halves[here, :128] = high
            halves[here, 128:] = (acc - high.astype(F32)).astype(BF16)
        return carry

    lax.fori_loop(0, CHUNKS, multiply, 0)
    ones = jnp.ones((16, 256), BF16)
    sums = lax.dot_general(ones, halves[...], (((1,), (1,)), ((), ())), preferred_element_type=F32)
    for c in range(8):
        mbuf[0, mp, c : c + 1, :] = sums[0:1, c * 128 : c * 128 + 128]
    mbuf[0, mp, 8:9, :] = jnp.zeros((1, 128), F32)

    pl.semaphore_wait(barrier, MP - 1 + DP - 1)
    scalar_blocks = [smbuf.at[pl.ds(0, MP - 1), pl.ds(0, SROWS)], sdbuf.at[pl.ds(0, DP - 1)]]

    def step(k, carry):
        now = lax.rem(k, 2)
        later = 1 - now

        mine = mbuf.at[now, mp, pl.ds(0, MROWS)]
        for peer in m_peers:
            pltpu.make_async_remote_copy(
                src_ref=mine, dst_ref=mine, send_sem=m_send.at[now], recv_sem=m_recv.at[now],
                device_id=peer, device_id_type=MESH,
            ).start()
        halo_copies = []
        for side, (first, peer) in enumerate(
            [(2, {"dp": dp, "mp": lax.rem(mp + 1, MP)}), (0, {"dp": dp, "mp": lax.rem(mp + MP - 1, MP)})]
        ):
            copy = pltpu.make_async_remote_copy(
                src_ref=ubuf.at[now, pl.ds(first, 2)], dst_ref=halo.at[now, side],
                send_sem=h_send.at[side], recv_sem=h_recv.at[now, side],
                device_id=peer, device_id_type=MESH,
            )
            copy.start()
            halo_copies.append(copy)

        def turn_some(low, high):
            row = lax.broadcasted_iota(jnp.int32, (256, 256), 0)
            col = lax.broadcasted_iota(jnp.int32, (256, 256), 1)
            eye = jnp.where(row == col, 1.0, 0.0).astype(BF16)

            def turn(j, carry):
                at = pl.multiple_of(j * 256, 256)
                turned = lax.dot_general(
                    eye, md[:, pl.ds(at, 256)], (((1,), (1,)), ((), ())), preferred_element_type=F32
                )
                mt[pl.ds(at, 256), :] = turned.astype(BF16)
                return carry

            lax.fori_loop(low, high, turn, 0)

        @pl.when(k == 0)
        def _():
            def arrange(j, carry):
                block = raw[pl.ds(pl.multiple_of(j * 2048, 2048), 2048), :].reshape(128, 16, 128)
                turned = jnp.swapaxes(block, 0, 1)
                for c in range(8):
                    for layer in range(2):
                        at = (layer * 8 + c) * 128
                        md[pl.ds(pl.multiple_of(j * 128, 128), 128), at : at + 128] = turned[c * 2 + layer]
                return carry

            lax.fori_loop(0, ROWS // 128, arrange, 0)
            turn_some(0, CELLS // 512)
            for small in smalls[1:]:
                small.wait()
            for layer in range(2):
                weight[layer] = smooth_ref[pl.ds(layer, 8, stride=2), :]
                for field in range(2):
                    at = pl.ds(field * 16 + layer, 8, stride=2)
                    free[layer * 2 + field] = 1.0 - active_ref[at, :].astype(F32)

        u = ubuf[now]
        mask = free[...]

        def regularize():
            for copy in halo_copies:
                copy.wait()
            below = jnp.where(mp > 0, halo[now, 0], 0.0)
            above = jnp.where(mp < MP - 1, halo[now, 1], 0.0)
            smooth = regular(u, below, above, weight[...])
            smooth_s[...] = smooth
            return smooth

        @pl.when(k == STEPS - 1)
        def _():
            smooth = regularize()
            r, s, rr, rs = r_s[...], s_s[...], rr_s[...], rs_s[...]
            pairs_of = [(r, r), (u, r), (s, r), (u, u), (u, s), (s, s), (r, rr), (u, rr), (s, rr), (u, smooth), (u, rs), (s, rs)]
            for j, (one, two) in enumerate(pairs_of):
                smbuf[mp, j : j + 1] = lanes_of(one * two)
            mine_s = smbuf.at[mp, pl.ds(0, SROWS)]
            for peer in m_peers:
                pltpu.make_async_remote_copy(
                    src_ref=mine_s, dst_ref=mine_s, send_sem=s_send.at[0], recv_sem=s_recv.at[0],
                    device_id=peer, device_id_type=MESH,
                ).start()

        all_m = mbuf.at[now, pl.ds(0, MP - 1), pl.ds(0, MROWS)]
        pltpu.make_async_copy(all_m, all_m, m_recv.at[now]).wait()
        rows = mbuf[now, 0, 0:8]
        sums = mbuf[now, 0, 8:9]
        for j in range(1, MP):
            rows += mbuf[now, j, 0:8]
            sums += mbuf[now, j, 8:9]

        scaled = rw_ref[...] * (rows - jnp.where(k == 0, obs_ref[...], 0.0))
        columns = product([scaled], md, CELLS - 512)
        dbuf[now, dp, 0:8] = gathered(columns[:8])
        dbuf[now, dp, 8:16] = gathered(columns[8:])
        mine_d = dbuf.at[now, dp]
        for peer in d_peers:
            pltpu.make_async_remote_copy(
                src_ref=mine_d, dst_ref=mine_d, send_sem=d_send.at[now], recv_sem=d_recv.at[now],
                device_id=peer, device_id_type=MESH,
            ).start()

        @pl.when(k < STEPS - 1)
        def _():
            regularize()

        @pl.when(k == 0)
        def _():
            turn_some(CELLS // 512, CELLS // 256)

        @pl.when(k == STEPS - 1)
        def _():
            fr, fs = fr_s[...], fs_s[...]
            for j, (one, two) in enumerate([(fr, fr), (rows, fr), (fs, fr), (rows, rows), (rows, fs), (fs, fs)]):
                sdbuf[dp, j : j + 1] = jnp.sum(rw_ref[...] * one * two, axis=0, keepdims=True)
            mine_e = sdbuf.at[dp]
            for peer in d_peers:
                pltpu.make_async_remote_copy(
                    src_ref=mine_e, dst_ref=mine_e, send_sem=s_send.at[1], recv_sem=s_recv.at[1],
                    device_id=peer, device_id_type=MESH,
                ).start()

        smooth = smooth_s[...]

        @pl.when(k == 0)
        def _():
            base[...] = -(mask * smooth)
            coef[...] = -mask

        @pl.when(k == 1)
        def _():
            r_s[...] = u
            fr_s[...] = rows
            rr_s[...] = smooth
            base[...] = mask * smooth
            coef[...] = mask

        @pl.when(k >= 2)
        def _():
            gamma, delta = split_sums(sums)
            first = k == 2
            beta = jnp.where(first, 0.0, gamma / jnp.where(first, 1.0, scal[0, 0:1, 0:1]))
            past = beta * gamma / jnp.where(first, 1.0, scal[1, 0:1, 0:1])
            alpha = gamma / (delta - past)
            scal[0] = jnp.broadcast_to(gamma, (8, 128))
            scal[1] = jnp.broadcast_to(alpha, (8, 128))
            scal[2] = jnp.broadcast_to(beta, (8, 128))
            r = r_s[...]
            p = r + beta * p_s[...]
            s = u + beta * s_s[...]
            r = r - alpha * s
            p_s[...] = p
            s_s[...] = s
            r_s[...] = r
            x_s[...] = x_s[...] + alpha * p
            fs = rows + beta * fs_s[...]
            fr = fr_s[...] - alpha * fs
            fs_s[...] = fs
            fr_s[...] = fr
            rs = smooth + beta * rs_s[...]
            rr = rr_s[...] - alpha * rs
            rs_s[...] = rs
            rr_s[...] = rr
            zb = mask * smooth + beta * z_s[...]
            z_s[...] = zb
            base[...] = u - alpha * zb
            coef[...] = -(alpha * mask)

        @pl.when(k == STEPS - 1)
        def _():
            for n, others in enumerate(scalar_blocks):
                pltpu.make_async_copy(others, others, s_recv.at[n]).wait()
            dots = smbuf[0, 0:SROWS]
            for j in range(1, MP):
                dots += smbuf[j, 0:SROWS]
            weighed = sdbuf[0]
            for j in range(1, DP):
                weighed += sdbuf[j]
            a, b, g = scal[1, 0:1, 0:1], scal[2, 0:1, 0:1], scal[0, 0:1, 0:1]

            def after(rows):
                rr, wr, sr, ww, ws, ss = (rows[j : j + 1] for j in range(6))
                terms = rr - (2.0 * a) * (wr + b * sr) + (a * a) * (ww + (2.0 * b) * ws + (b * b) * ss)
                return jnp.sum(terms, axis=1, keepdims=True)

            gamma = after(dots[0:6])
            delta = after(dots[6:12]) + after(weighed[0:6])
            beta = gamma / g
            alpha = gamma / (delta - beta * gamma / a)
            r = r_s[...]
            upd = x_s[...] + alpha * (r + beta * p_s[...])
            base[...] = r - alpha * (beta * s_s[...] + base[...])
            coef[...] = -(alpha * coef[...])
            for layer in range(2):
                for field in range(2):
                    out_ref[0, pl.ds(field * 16 + layer, 8, stride=2), :] = upd[layer * 2 + field]

        pltpu.make_async_copy(all_m, all_m, m_send.at[now]).wait()
        all_d = dbuf.at[now, pl.ds(0, DP - 1)]
        pltpu.make_async_copy(all_d, all_d, d_recv.at[now]).wait()
        density = dbuf[now, 0]
        for j in range(1, 6):
            density += dbuf[now, j]
        suscept = dbuf[now, 6] + dbuf[now, 7]
        summed = jnp.stack([density[:8], suscept[:8], density[8:], suscept[8:]])
        v = base[...] + coef[...] * summed
        ubuf[later] = v
        z_s[...] = z_s[...] + jnp.where(k >= 2, mask, 0.0) * summed

        @pl.when(k < STEPS - 1)
        def _():
            mbuf[later, mp, 0:8] = gathered(product(chosen(v), mt, ROWS - 256))
            r = r_s[...]
            mbuf[later, mp, 8:9] = two_sums(lanes_of(r * r), lanes_of(r * v))

        pltpu.make_async_copy(all_d, all_d, d_send.at[now]).wait()
        return carry

    r_s[...] = jnp.zeros_like(r_s)
    lax.fori_loop(0, STEPS, step, 0)

    res = ubuf[STEPS % 2]
    for layer in range(2):
        for field in range(2):
            out_ref[1, pl.ds(field * 16 + layer, 8, stride=2), :] = res[layer * 2 + field]
    for n, others in enumerate(scalar_blocks):
        pltpu.make_async_copy(others, others, s_send.at[n]).wait()


def pairs(field):
    lead = field.shape[:-2]
    n = len(lead)
    cut = field.reshape(*lead, 2, 8, 128)
    return jnp.swapaxes(cut, n, n + 1).reshape(-1, 128)


def unpairs(rows):
    return jnp.swapaxes(rows.reshape(2, 2, 8, 2, 128), 2, 3).reshape(2, 2, 2, 1024)


def local(sensitivity, observed, row_weight, model, smooth_weight, active):
    vmem = pl.BlockSpec(memory_space=pltpu.VMEM)
    cells = pltpu.VMEM((4, 8, 128), F32)
    tile = pltpu.VMEM((8, 128), F32)
    out = pl.pallas_call(
        kernel,
        out_shape=jax.ShapeDtypeStruct((2, 32, 128), F32),
        in_specs=[pl.BlockSpec(memory_space=pltpu.HBM)] * 6,
        out_specs=vmem,
        scratch_shapes=[
            tile, tile,
            pltpu.VMEM((32, 128), F32),
            pltpu.VMEM((16, 128), F32),
            pltpu.VMEM((32, 128), jnp.int32),
            pltpu.VMEM((ROWS * 16, 128), BF16),
            pltpu.VMEM((ROWS, 256), BF16),
            pltpu.VMEM((ROWS, CELLS), BF16),
            pltpu.VMEM((CELLS, ROWS), BF16),
            pltpu.VMEM((2, MP, 16, 128), F32),
            pltpu.VMEM((2, DP, 16, 128), F32),
            pltpu.VMEM((2, 4, 8, 128), F32),
            pltpu.VMEM((2, 2, 2, 8, 128), F32),
            pltpu.VMEM((MP, 16, 128), F32),
            pltpu.VMEM((DP, 8, 128), F32),
            cells,
            pltpu.VMEM((2, 8, 128), F32),
            cells, cells, cells, cells, cells, cells, cells, cells, cells, cells,
            tile, tile,
            pltpu.VMEM((3, 8, 128), F32),
            pltpu.SemaphoreType.DMA((5,)),
            pltpu.SemaphoreType.DMA((CHUNKS,)),
            pltpu.SemaphoreType.DMA((2,)),
            pltpu.SemaphoreType.DMA((2,)),
            pltpu.SemaphoreType.DMA((2,)),
            pltpu.SemaphoreType.DMA((2,)),
            pltpu.SemaphoreType.DMA((2,)),
            pltpu.SemaphoreType.DMA((2, 2)),
            pltpu.SemaphoreType.DMA((2,)),
            pltpu.SemaphoreType.DMA((2,)),
        ],
        compiler_params=pltpu.CompilerParams(
            collective_id=0, has_side_effects=True, vmem_limit_bytes=32 * 2**20
        ),
    )(
        *(
            pltpu.with_memory_space_constraint(x, pltpu.HBM)
            for x in (
                pairs(sensitivity),
                observed.reshape(8, 128),
                row_weight.reshape(8, 128),
                pairs(model),
                pairs(smooth_weight),
                pairs(active),
            )
        )
    )
    both = unpairs(out)
    return both[0], both[1]


def solution(mesh):
    return jax.shard_map(
        local,
        mesh=mesh,
        in_specs=(
            P("dp", "mp", None),
            P("dp"),
            P("dp"),
            P(None, "mp", None),
            P("mp", None),
            P(None, "mp", None),
        ),
        out_specs=(P(None, "mp", None), P(None, "mp", None)),
        check_vma=False,
    )
```
